256 devices in a mesh: row: 16 (over y, z_hi), col: 16 (over x, z_lo, core).
Axes of the slice: x: 4, y: 4, z: 8 (z_hi: 4, z_lo: 2; z = z_hi * 2 + z_lo), core: 2. Of those that a mesh axis runs over, the one named last changes fastest.
Arguments:
- inputs: bfloat16 [131072, 256], P(('row', 'col')), may hold values from -6 to 6
- aggregated: bfloat16 [131072, 256], P(('row', 'col')), may hold values from -6 to 6
- grad_out: bfloat16 [131072, 256], P(('row', 'col')), may hold values from -6 to 6
- preact: bfloat16 [131072, 256], P(('row', 'col')), may hold values from -6 to 6
- inv_degree: bfloat16 [131072], P(('row', 'col')), may hold values from 0.099609375 to 1
- w_self: bfloat16 [256, 256], replicated, may hold values from -0.375 to 0.375
- w_neigh: bfloat16 [256, 256], replicated, may hold values from -0.375 to 0.375
- blocks: bfloat16 [86016, 128, 128], P(('row', 'col')), may hold values from 0 to 0.079589844
- block_rows: int32 [86016], P(('row', 'col')), may hold values from 0 to 63
- block_cols: int32 [86016], P(('row', 'col')), may hold values from 0 to 63
- block_count: int32 [16, 16], P('row', 'col'), may hold values from 42 to 336, as said below
Outputs:
- grad_inputs: bfloat16 [131072, 256], P(('row', 'col'))
- grad_self: float32 [256, 256], replicated
- grad_neigh: float32 [256, 256], replicated
- grad_bias: float32 [256], replicated
The draws below stay inside these ranges and needn't reach their ends.
Inputs may be any that keep to these rules, and one draw needn't show every extreme that they name: `block_count`: some grid cell has exactly 336 live slots.
All inputs are finite; a program needn't handle non-finite values.
Results may differ from the reference program's by a relative error of at most 0.015.
Values may be sent and summed in bfloat16 or wider, within the bound.
A program may use at most 128 MiB of HBM per device.

```python
import math
import jax
import jax.numpy as jnp
from jax import lax

FEAT_IN = 256
FEAT_OUT = 256
BLOCK = 128
ROWS_DEV = 512
NB_MAX = 336
NODES = 131072
N_ROW = 16
N_COL = 16


def slot_pattern(key):
    slot_total = N_ROW * N_COL * NB_MAX
    tile_count = ROWS_DEV // BLOCK
    key_list = jax.random.split(key, 6)
    slot_index = jnp.arange(slot_total, dtype=jnp.int32)
    cell_index = slot_index // NB_MAX
    grid_row = cell_index // N_COL
    grid_col = cell_index % N_COL
    slot_kind = jax.random.randint(key_list[0], (slot_total,), 0, 4, dtype=jnp.int32)
    inner_row = jax.random.randint(key_list[1], (slot_total,), 0, tile_count, dtype=jnp.int32)
    inner_col = jax.random.randint(key_list[2], (slot_total,), 0, tile_count, dtype=jnp.int32)
    offset_table = jnp.array([-2, -1, 1, 2], dtype=jnp.int32)
    offsets = offset_table[jax.random.randint(key_list[3], (slot_total,), 0, 4, dtype=jnp.int32)]
    tail_row = jax.random.randint(key_list[4], (slot_total,), 0, ROWS_DEV * N_COL // BLOCK, dtype=jnp.int32)
    tail_col = jax.random.randint(key_list[5], (slot_total,), 0, ROWS_DEV * N_ROW // BLOCK, dtype=jnp.int32)
    near_row = grid_col * tile_count + inner_row
    band_cell = (grid_row + offsets) % N_ROW
    near_col = jnp.where(slot_kind == 2, band_cell, grid_row) * tile_count + inner_col
    rows_out = jnp.where(slot_kind == 3, tail_row, near_row).astype(jnp.int32)
    cols_out = jnp.where(slot_kind == 3, tail_col, near_col).astype(jnp.int32)
    return (rows_out, cols_out)


def draw_block_rows(key, part):
    rows_out, cols_out = slot_pattern(key)
    return rows_out


def draw_block_cols(key, part):
    rows_out, cols_out = slot_pattern(key)
    return cols_out


def draw_block_count(key, part):
    key = jax.random.fold_in(key, 37)
    first_key, second_key = jax.random.split(key)
    exponents = jax.random.randint(first_key, (N_ROW * N_COL,), 0, 4, dtype=jnp.int32)
    counts = NB_MAX // jnp.left_shift(jnp.ones_like(exponents), exponents)
    chosen = jax.random.randint(second_key, (), 0, N_ROW * N_COL, dtype=jnp.int32)
    counts = jnp.where(jnp.arange(N_ROW * N_COL, dtype=jnp.int32) == chosen, NB_MAX, counts)
    return counts.astype(jnp.int32).reshape(N_ROW, N_COL)


def shard_levels(stream_key, extent, cuts, smallest, largest):
    def one(axis_at, parts):
        heights = jax.random.uniform(jax.random.fold_in(jax.random.fold_in(stream_key, 6), axis_at), (parts,), jnp.float32, smallest / len(cuts), largest / len(cuts))
        return jnp.repeat(jnp.exp(heights), extent[axis_at] // parts).reshape((-1,) + (1,) * (len(extent) - axis_at - 1))

    factor_of = one(*cuts[0])
    for cut in cuts[1:]:
        factor_of = factor_of * one(*cut)
    return factor_of


def scatter_about(key, shape, spread, reach, pieces=(), kind=jnp.bfloat16):
    result = jax.random.normal(key, shape, jnp.float32) * spread
    if len(pieces) > 0:
        result = shard_levels(key, shape, pieces, -0.22, 0.18) * result
    return jnp.clip(result, min=-reach, max=reach).astype(kind)


def setup_inputs(seed: int = 0) -> dict:
    keys = jax.random.split(jax.random.key(seed), 12)
    return {
        "inputs": scatter_about(keys[0], (NODES, FEAT_IN), 1.0, 6.0, ((0, 256),)),
        "aggregated": scatter_about(keys[1], (NODES, FEAT_IN), 1.0, 6.0, ((0, 256),)),
        "grad_out": scatter_about(keys[2], (NODES, FEAT_OUT), 1.0, 6.0, ((0, 256),)),
        "preact": scatter_about(keys[3], (NODES, FEAT_OUT), 1.0, 6.0, ((0, 256),)),
        "inv_degree": jnp.clip(jnp.exp(math.log(1.0) - 2.306499 * jax.random.uniform(keys[4], (NODES,), jnp.float32) ** shard_levels(keys[4], (NODES,), ((0, 256),), -0.2, 0.2)), 0.099609375, 1.0).astype(jnp.bfloat16),
        "w_self": scatter_about(keys[5], (FEAT_IN, FEAT_OUT), FEAT_IN ** -0.5, 0.375),
        "w_neigh": scatter_about(keys[6], (FEAT_IN, FEAT_OUT), FEAT_IN ** -0.5, 0.375),
        "blocks": jnp.clip(0.079589844 * jax.random.uniform(keys[7], (N_ROW * N_COL * NB_MAX, BLOCK, BLOCK), jnp.float32) ** shard_levels(keys[7], (N_ROW * N_COL * NB_MAX, BLOCK, BLOCK), ((0, 256),), -0.2, 0.2), 0.0, 0.079589844).astype(jnp.bfloat16),
        "block_rows": draw_block_rows(jax.random.fold_in(keys[11], 71), 0),
        "block_cols": draw_block_cols(jax.random.fold_in(keys[11], 71), 0),
        "block_count": draw_block_count(jax.random.fold_in(keys[11], 71), 0),
    }


def reference(inputs, aggregated, grad_out, preact, inv_degree, w_self, w_neigh, blocks, block_rows, block_cols, block_count):
    masked = jnp.where(preact > 0, grad_out, jnp.zeros_like(grad_out))
    projected = jnp.dot(masked, w_neigh.T, preferred_element_type=jnp.float32)
    neigh_grads = (projected * inv_degree.astype(jnp.float32)[:, None]).astype(jnp.bfloat16)
    self_term = jnp.dot(masked, w_self.T, preferred_element_type=jnp.float32)
    strip_len = ROWS_DEV * N_COL
    group_len = ROWS_DEV * N_ROW
    cells = N_ROW * N_COL
    slot_values = blocks.reshape(cells, NB_MAX, BLOCK, BLOCK)
    slot_rows = block_rows.reshape(cells, NB_MAX)
    slot_cols = block_cols.reshape(cells, NB_MAX)
    counts = block_count.reshape(cells)

    def one_device(totals, packed):
        values, row_ids, col_ids, live_count, device = packed
        grid_row = device // N_COL
        grid_col = device % N_COL
        start = (grid_row * strip_len).astype(jnp.int32)
        strip = lax.dynamic_slice_in_dim(neigh_grads, start, strip_len, 0)
        strip = strip.reshape(strip_len // BLOCK, BLOCK, FEAT_IN)
        picked = strip[row_ids]
        product = jnp.einsum("kij,kif->kjf", values.astype(jnp.float32), picked.astype(jnp.float32))
        active = jnp.arange(NB_MAX, dtype=jnp.int32) < live_count
        product = jnp.where(active[:, None, None], product, jnp.zeros_like(product))
        partial_value = jnp.zeros((group_len // BLOCK, BLOCK, FEAT_IN), jnp.float32).at[col_ids].add(product)
        current = lax.dynamic_index_in_dim(totals, grid_col, 0, keepdims=False)
        totals = lax.dynamic_update_index_in_dim(totals, current + partial_value.reshape(group_len, FEAT_IN), grid_col, 0)
        return totals, None

    totals = jnp.zeros((N_COL, group_len, FEAT_IN), jnp.float32)
    totals, unused = lax.scan(one_device, totals, (slot_values, slot_rows, slot_cols, counts, jnp.arange(cells, dtype=jnp.int32)))
    neighbour = totals.reshape(N_COL, N_ROW, ROWS_DEV, FEAT_IN).transpose(1, 0, 2, 3).reshape(NODES, FEAT_IN)
    grad_inputs = (self_term + neighbour).astype(jnp.bfloat16)
    grad_self = jnp.dot(inputs.T, masked, preferred_element_type=jnp.float32)
    grad_neigh = jnp.dot(aggregated.T, masked, preferred_element_type=jnp.float32)
    grad_bias = jnp.sum(masked.astype(jnp.float32), axis=0)
    return (grad_inputs, grad_self, grad_neigh, grad_bias)
```

```python
import functools

import jax
import jax.numpy as jnp
from jax import lax
from jax.experimental import pallas as pl
from jax.experimental.pallas import tpu as pltpu
from jax.sharding import PartitionSpec as P

EDGE = 128
F32 = jnp.float32
BF16 = jnp.bfloat16
FLOWS = (("y", "z", 0, 384), ("z", "y", 384, 128))
SHARE = 32
SHARE_PAD = 40


def place():
    r = lax.axis_index("row")
    c = lax.axis_index("col")
    return r // 4, r % 4, c // 4, (c // 2) % 2, c % 2


def device(y, z, x, pair, core):
    return {"row": y * 4 + z, "col": x * 4 + pair * 2 + core}


def greet(peers):
    barrier = pltpu.get_barrier_semaphore()
    for peer in peers:
        pl.semaphore_signal(barrier, inc=1, device_id=peer, device_id_type=pl.DeviceIdType.MESH)
    pl.semaphore_wait(barrier, len(peers))


class Post:
    def __init__(self, send_sem, recv_sem):
        self.send_sem = send_sem
        self.recv_sem = recv_sem
        self.sent = []

    def send(self, src, dst, peer):
        at = len(self.sent)
        copy = pltpu.make_async_remote_copy(
            src_ref=src,
            dst_ref=dst,
            send_sem=self.send_sem.at[at],
            recv_sem=self.recv_sem.at[at],
            device_id=peer,
            device_id_type=pl.DeviceIdType.MESH,
        )
        copy.start()
        self.sent.append(copy)
        return copy

    def finish(self):
        for copy in self.sent:
            copy.wait_send()


def gather_kernel(
    inputs, aggregated, grad_out, preact, inv, w_self, w_neigh,
    strip_out, self_term, shares, strip, masked_ref, send_sem, recv_sem, out_sem,
):
    y, z, x, pair, core = place()
    rows = inputs.shape[0]
    half = rows // 2
    right, left, opposite, other = (x + 1) % 4, (x + 3) % 4, (x + 2) % 4, 1 - pair
    to_right = device(y, z, right, pair, core)
    to_left = device(y, z, left, pair, core)
    to_pair = device(y, z, x, other, core)
    to_core = device(y, z, x, pair, 1 - core)
    greet((to_right, to_left, to_pair, to_core))
    post = Post(send_sem, recv_sem)
    stored = []

    def part(at_x, at_pair, at_core, h):
        shard = (at_x * 2 + at_pair) * 2 + at_core
        return pl.ds(pl.multiple_of(shard * rows + h * half, half), half)

    def send(where, peer):
        return post.send(strip.at[where], strip.at[where], peer)

    def store(where):
        copy = pltpu.make_async_copy(strip.at[where], strip_out.at[where], out_sem.at[len(stored)])
        copy.start()
        stored.append(copy)

    eye = lax.broadcasted_iota(jnp.int32, (EDGE, EDGE), 0) == lax.broadcasted_iota(
        jnp.int32, (EDGE, EDGE), 1
    )
    own_right, own_left, own_pair, own_core = {}, {}, {}, {}
    for h in range(2):
        base = h * half
        grads = grad_out[base : base + half, :]
        masked = jnp.where(preact[base : base + half, :] > 0, grads, jnp.zeros_like(grads))
        masked_ref[base : base + half, :] = masked
        projected = lax.dot_general(
            masked, w_neigh[...], (((1,), (1,)), ((), ())), preferred_element_type=F32
        )
        for t in range(half // EDGE):
            at = h * (half // EDGE) + t
            row = jnp.broadcast_to(inv[at : at + 1, :], (EDGE, EDGE))
            scale = jnp.sum(jnp.where(eye, row, jnp.zeros_like(row)), axis=1, keepdims=True)
            shard = (x * 2 + pair) * 2 + core
            place_at = pl.ds(pl.multiple_of(shard * rows + at * EDGE, EDGE), EDGE)
            strip[place_at, :] = (projected[t * EDGE : (t + 1) * EDGE, :] * scale).astype(BF16)
        mine = part(x, pair, core, h)
        own_right[h] = send(mine, to_right)
        own_left[h] = send(mine, to_left)
        own_pair[h] = send(mine, to_pair)
        own_core[h] = send(mine, to_core)
        store(mine)

    masked = masked_ref[...]
    self_term[...] = lax.dot_general(
        masked, w_self[...], (((1,), (1,)), ((), ())), preferred_element_type=F32
    )
    bias = jnp.sum(masked.astype(F32), axis=0, keepdims=True)
    count = shares.shape[0] // 2
    for which, left_side in enumerate((inputs, aggregated)):
        product = lax.dot_general(
            left_side[...], masked, (((0,), (0,)), ((), ())), preferred_element_type=F32
        )
        for q in range(count):
            shares[which * count + q, :SHARE, :] = product[q * SHARE : (q + 1) * SHARE, :]
            shares[which * count + q, SHARE:, :] = jnp.broadcast_to(
                bias, (SHARE_PAD - SHARE, bias.shape[1])
            )

    passed = []

    def arrived(copy, spot):
        copy.wait_recv()
        at_x, at_pair, h = spot
        where = part(at_x, at_pair, core, h)
        passed.append((send(where, to_core), part(at_x, at_pair, 1 - core, h)))
        store(where)
        return where

    for h in range(2):
        passed.append((own_core[h], part(x, pair, 1 - core, h)))
    where = arrived(own_right[0], (left, pair, 0))
    far_0 = send(where, to_right)
    where = arrived(own_left[0], (right, pair, 0))
    where = arrived(own_pair[0], (x, other, 0))
    other_right_0 = send(where, to_right)
    other_left_0 = send(where, to_left)
    where = arrived(own_left[1], (right, pair, 1))
    far_1 = send(where, to_left)
    where = arrived(own_right[1], (left, pair, 1))
    where = arrived(own_pair[1], (x, other, 1))
    other_right_1 = send(where, to_right)
    other_left_1 = send(where, to_left)
    where = arrived(far_0, (opposite, pair, 0))
    far_pair_0 = send(where, to_pair)
    where = arrived(far_1, (opposite, pair, 1))
    far_pair_1 = send(where, to_pair)
    arrived(other_right_0, (left, other, 0))
    arrived(other_left_0, (right, other, 0))
    arrived(other_right_1, (left, other, 1))
    arrived(other_left_1, (right, other, 1))
    arrived(far_pair_0, (opposite, other, 0))
    arrived(far_pair_1, (opposite, other, 1))
    for copy, where in passed:
        copy.wait_recv()
        store(where)
    for copy in stored:
        copy.wait()
    post.finish()


def spmm_kernel(
    rows_ref, cols_ref, count_ref, blocks, strip_in, out, strip, total, ring, ring_sem, strip_sem
):
    depth, chunk = ring.shape[0], ring.shape[1]
    group = 16
    live_count = count_ref[0]
    chunks = lax.div(live_count + chunk - 1, chunk)
    strip_copy = pltpu.make_async_copy(strip_in, strip, strip_sem)
    strip_copy.start()

    def fetch(at, slot):
        return pltpu.make_async_copy(
            blocks.at[pl.ds(at * chunk, chunk)], ring.at[slot], ring_sem.at[slot]
        )

    for at in range(depth - 1):

        @pl.when(at < chunks)
        def _():
            fetch(at, at).start()

    tall = 256

    def clear(t, carry):
        total[pl.ds(pl.multiple_of(t * tall, tall), tall), :] = jnp.zeros(
            (tall, total.shape[1]), F32
        )
        return carry

    lax.fori_loop(0, total.shape[0] // tall, clear, 0)
    strip_copy.wait()

    def one(at, slot, inner):
        r = pl.multiple_of(rows_ref[at] * EDGE, EDGE)
        c = pl.multiple_of(cols_ref[at] * EDGE, EDGE)
        total[pl.ds(c, EDGE), :] += lax.dot_general(
            ring[slot, inner],
            strip[pl.ds(r, EDGE), :],
            (((0,), (0,)), ((), ())),
            preferred_element_type=F32,
        )

    def step(at, carry):
        slot = lax.rem(at, depth)
        ahead = at + depth - 1

        @pl.when(ahead < chunks)
        def _():
            fetch(ahead, lax.rem(ahead, depth)).start()

        fetch(at, slot).wait()
        live = jnp.minimum(live_count - at * chunk, chunk)
        groups = lax.div(live, group)

        def many(u, carry):
            for i in range(group):
                one(at * chunk + u * group + i, slot, u * group + i)
            return carry

        lax.fori_loop(0, groups, many, 0)

        def rest(i, carry):
            one(at * chunk + i, slot, i)
            return carry

        lax.fori_loop(groups * group, live, rest, 0)
        return carry

    lax.fori_loop(0, chunks, step, 0)

    def leave(t, carry):
        span = pl.ds(pl.multiple_of(t * tall, tall), tall)
        out[span, :] = total[span, :].astype(BF16)
        return carry

    lax.fori_loop(0, total.shape[0] // tall, leave, 0)


def reduce_kernel(partial, self_term, shares, out, weights, bias, *scratch):
    flow_refs = [scratch[i * 7 : i * 7 + 7] for i in range(len(FLOWS))]
    from_core, from_pair, from_x, from_y, from_z, work_a, work_b, work_c, work_d, work_e = scratch[14:24]
    send_sem, recv_sem = scratch[24:26]
    y, z, x, pair, core = place()
    rows = self_term.shape[0]
    turn = lambda v, by: (v + by) % 4
    peer_y = {by: device(turn(y, by), z, x, pair, core) for by in (1, 2, 3)}
    peer_z = {by: device(y, turn(z, by), x, pair, core) for by in (1, 2, 3)}
    peer_x = {by: device(y, z, turn(x, by), pair, core) for by in (1, 2, 3)}
    to_pair = device(y, z, x, 1 - pair, core)
    to_core = device(y, z, x, pair, 1 - core)
    greet(
        [peer[by] for peer in (peer_y, peer_z, peer_x) for by in (1, 2, 3)] + [to_pair, to_core]
    )
    post = Post(send_sem, recv_sem)
    peers = {"y": peer_y, "z": peer_z}
    own = {"y": y, "z": z}

    def flow(refs, first, second, offset, span):
        via_a, left_a, right_a, sum_a, hold, via_b, side_b = refs
        h = span // 2
        halves = (slice(0, h), slice(h, span))
        ahead_a, back_a = peers[first][1], peers[first][3]
        ahead_b, back_b = peers[second][1], peers[second][3]
        order = (2, 1, 3, 0)

        def piece(by_a, by_b, k):
            at = {first: turn(own[first], by_a), second: turn(own[second], by_b)}
            start = (at["y"] * 4 + at["z"]) * rows + offset
            if k is None:
                return pl.ds(pl.multiple_of(start, 16), span)
            return pl.ds(pl.multiple_of(start + k * h, 16), h)

        far, near = {}, {}

        def launch(i):
            b = order[i]
            far[i] = (
                post.send(partial.at[piece(2, b, 0)], via_a.at[i, 0], ahead_a),
                post.send(partial.at[piece(2, b, 1)], via_a.at[i, 1], back_a),
            )
            near[i] = [
                post.send(partial.at[piece(1, b, 1)], left_a.at[i, pl.ds(h, h)], ahead_a),
                post.send(partial.at[piece(3, b, 0)], right_a.at[i, pl.ds(0, h)], back_a),
            ]

        def relay(i):
            b = order[i]
            far[i][0].wait_recv()
            sum_a[i, 0] = (
                via_a[i, 0].astype(F32) + partial[piece(1, b, 0), :].astype(F32)
            ).astype(BF16)
            near[i].append(post.send(sum_a.at[i, 0], left_a.at[i, pl.ds(0, h)], ahead_a))
            far[i][1].wait_recv()
            sum_a[i, 1] = (
                via_a[i, 1].astype(F32) + partial[piece(3, b, 1), :].astype(F32)
            ).astype(BF16)
            near[i].append(post.send(sum_a.at[i, 1], right_a.at[i, pl.ds(h, h)], back_a))

        def close(i):
            for copy in near[i]:
                copy.wait_recv()
            return (
                partial[piece(0, order[i], None), :].astype(F32)
                + left_a[i].astype(F32)
                + right_a[i].astype(F32)
            )

        launch(0)
        launch(1)
        yield
        sent_b = []
        for i in range(5):
            if i < 4:
                relay(i)
                if i + 2 < 4:
                    launch(i + 2)
                yield
            if i == 0:
                continue
            done = close(i - 1)
            if i == 1:
                hold[0] = done.astype(BF16)
                far_b = (
                    post.send(hold.at[0, pl.ds(0, h)], via_b.at[0], ahead_b),
                    post.send(hold.at[0, pl.ds(h, h)], via_b.at[1], back_b),
                )
            elif i == 2:
                hold[1, pl.ds(h, h), :] = done[halves[1], :].astype(BF16)
                sent_b.append(
                    post.send(hold.at[1, pl.ds(h, h)], side_b.at[0, pl.ds(h, h)], ahead_b)
                )
                far_b[0].wait_recv()
                hold[1, pl.ds(0, h), :] = (done[halves[0], :] + via_b[0].astype(F32)).astype(BF16)
                sent_b.append(
                    post.send(hold.at[1, pl.ds(0, h)], side_b.at[0, pl.ds(0, h)], ahead_b)
                )
            elif i == 3:
                hold[2, pl.ds(0, h), :] = done[halves[0], :].astype(BF16)
                sent_b.append(
                    post.send(hold.at[2, pl.ds(0, h)], side_b.at[1, pl.ds(0, h)], back_b)
                )
                far_b[1].wait_recv()
                hold[2, pl.ds(h, h), :] = (done[halves[1], :] + via_b[1].astype(F32)).astype(BF16)
                sent_b.append(
                    post.send(hold.at[2, pl.ds(h, h)], side_b.at[1, pl.ds(h, h)], back_b)
                )
            else:
                done = done + self_term[pl.ds(offset, span), :]
                yield
                for copy in sent_b:
                    copy.wait_recv()
                out[pl.ds(offset, span), :] = (
                    done + side_b[0].astype(F32) + side_b[1].astype(F32)
                ).astype(BF16)
            yield

    def weight_sums():
        eight, four = shares.shape[0] // 2, shares.shape[0] // 4
        copy = post.send(shares.at[pl.ds((1 - core) * eight, eight)], from_core, to_core)
        yield
        copy.wait_recv()
        work_a[...] = shares[pl.ds(core * eight, eight)] + from_core[...]
        copy = post.send(work_a.at[pl.ds((1 - pair) * four, four)], from_pair, to_pair)
        yield
        copy.wait_recv()
        work_b[...] = work_a[pl.ds(pair * four, four)] + from_pair[...]
        copies = [
            post.send(work_b.at[turn(x, by)], from_x.at[by - 1], peer_x[by]) for by in (1, 2, 3)
        ]
        yield
        for copy in copies:
            copy.wait_recv()
        work_c[...] = work_b[x] + from_x[0] + from_x[1] + from_x[2]
        from_y[y] = work_c[...]
        copies = [post.send(work_c, from_y.at[y], peer_y[by]) for by in (1, 2, 3)]
        yield
        for copy in copies:
            copy.wait_recv()
        work_d[...] = from_y[0] + from_y[1] + from_y[2] + from_y[3]
        from_z[z] = work_d[...]
        copies = [post.send(work_d, from_z.at[z], peer_z[by]) for by in (1, 2, 3)]
        yield
        for copy in copies:
            copy.wait_recv()
        work_e[...] = from_z[0] + from_z[1] + from_z[2] + from_z[3]
        bias[...] = work_e[pl.ds(SHARE, SHARE_PAD - SHARE), :]
        mine = core * eight + pair * four + x

        def span(first, count):
            return pl.ds(pl.multiple_of(first * SHARE, SHARE), count * SHARE)

        weights[span(mine, 1), :] = work_e[pl.ds(0, SHARE), :]
        copies = [
            post.send(work_e.at[pl.ds(0, SHARE)], weights.at[span(mine, 1)], peer_x[by])
            for by in (1, 2, 3)
        ]
        yield
        for copy in copies:
            copy.wait_recv()
        where = span(core * eight + pair * four, four)
        copy = post.send(weights.at[where], weights.at[where], to_pair)
        yield
        copy.wait_recv()
        where = span(core * eight, eight)
        copy = post.send(weights.at[where], weights.at[where], to_core)
        yield
        copy.wait_recv()

    turns = [flow(refs, *spec) for refs, spec in zip(flow_refs, FLOWS)] + [weight_sums()]
    while turns:
        for one in list(turns):
            try:
                next(one)
            except StopIteration:
                turns.remove(one)
    post.finish()


def local(
    inputs, aggregated, grad_out, preact, inv_degree, w_self, w_neigh,
    blocks, block_rows, block_cols, block_count,
):
    rows, feat = inputs.shape
    strip_rows = rows * lax.axis_size("col")
    group_rows = rows * lax.axis_size("row")
    vmem = pl.BlockSpec(memory_space=pltpu.VMEM)
    anywhere = pl.BlockSpec(memory_space=pl.ANY)
    dma = pltpu.SemaphoreType.DMA
    inv = inv_degree.astype(F32).reshape(rows // EDGE, EDGE)
    strip, self_term, shares = pl.pallas_call(
        gather_kernel,
        out_shape=(
            jax.ShapeDtypeStruct((strip_rows, feat), BF16),
            jax.ShapeDtypeStruct((rows, feat), F32),
            jax.ShapeDtypeStruct((16, SHARE_PAD, feat), F32),
        ),
        in_specs=[vmem] * 7,
        out_specs=(anywhere, vmem, vmem),
        scratch_shapes=[
            pltpu.VMEM((strip_rows, feat), BF16),
            pltpu.VMEM((rows, feat), BF16),
            dma((30,)),
            dma((30,)),
            dma((32,)),
        ],
        compiler_params=pltpu.CompilerParams(
            collective_id=0, has_side_effects=True, vmem_limit_bytes=32 * 2**20
        ),
        name="gather",
    )(inputs, aggregated, grad_out, preact, inv, w_self, w_neigh)

    depth, chunk = 4, 16
    partial = pl.pallas_call(
        spmm_kernel,
        out_shape=jax.ShapeDtypeStruct((group_rows, feat), BF16),
        grid_spec=pltpu.PrefetchScalarGridSpec(
            num_scalar_prefetch=3,
            grid=(1,),
            in_specs=[anywhere, anywhere],
            out_specs=pl.BlockSpec((group_rows, feat), lambda i, *unused: (0, 0)),
            scratch_shapes=[
                pltpu.VMEM((strip_rows, feat), BF16),
                pltpu.VMEM((group_rows, feat), F32),
                pltpu.VMEM((depth, chunk, EDGE, EDGE), BF16),
                dma((depth,)),
                dma,
            ],
        ),
        compiler_params=pltpu.CompilerParams(vmem_limit_bytes=40 * 2**20),
        name="spmm",
    )(block_rows, block_cols, block_count.reshape(1), blocks, strip)

    scratch = []
    for unused_a, unused_b, unused_c, span in FLOWS:
        scratch += [
            pltpu.VMEM((4, 2, span // 2, feat), BF16),
            pltpu.VMEM((4, span, feat), BF16),
            pltpu.VMEM((4, span, feat), BF16),
            pltpu.VMEM((4, 2, span // 2, feat), BF16),
            pltpu.VMEM((3, span, feat), BF16),
            pltpu.VMEM((2, span // 2, feat), BF16),
            pltpu.VMEM((2, span, feat), BF16),
        ]
    share = (SHARE_PAD, feat)
    scratch += [
        pltpu.VMEM((8,) + share, F32),
        pltpu.VMEM((4,) + share, F32),
        pltpu.VMEM((3,) + share, F32),
        pltpu.VMEM((4,) + share, F32),
        pltpu.VMEM((4,) + share, F32),
        pltpu.VMEM((8,) + share, F32),
        pltpu.VMEM((4,) + share, F32),
        pltpu.VMEM(share, F32),
        pltpu.VMEM(share, F32),
        pltpu.VMEM(share, F32),
        dma((2 * 30 + 16,)),
        dma((2 * 30 + 16,)),
    ]
    grad_inputs, weights, bias = pl.pallas_call(
        reduce_kernel,
        out_shape=(
            jax.ShapeDtypeStruct((rows, feat), BF16),
            jax.ShapeDtypeStruct((16 * SHARE, feat), F32),
            jax.ShapeDtypeStruct((SHARE_PAD - SHARE, feat), F32),
        ),
        in_specs=[vmem] * 3,
        out_specs=(vmem, vmem, vmem),
        scratch_shapes=scratch,
        compiler_params=pltpu.CompilerParams(
            collective_id=1, has_side_effects=True, vmem_limit_bytes=32 * 2**20
        ),
        name="reduce",
    )(partial, self_term, shares)
    return grad_inputs, weights[:feat], weights[feat:], bias[0]


def solution(mesh):
    both = ("row", "col")
    return jax.shard_map(
        local,
        mesh=mesh,
        in_specs=(
            P(both, None), P(both, None), P(both, None), P(both, None), P(both),
            P(), P(),
            P(both, None, None), P(both), P(both), P("row", "col"),
        ),
        out_specs=(P(both, None), P(), P(), P()),
        check_vma=False,
    )
```

```python
import functools

import jax
import jax.numpy as jnp
from jax import lax
from jax.experimental import pallas as pl
from jax.experimental.pallas import tpu as pltpu
from jax.sharding import PartitionSpec as P

EDGE = 128
HALVES = 2
TILES = 64
I32 = jnp.int32
F32 = jnp.float32
BF16 = jnp.bfloat16
FLOWS = (("y", "z", 0, 384), ("z", "y", 384, 128))
PAD = 8
LIMIT = 62
PAIRS = 200
STRIDE = 20
PART = 40


def place():
    r = lax.axis_index("row")
    c = lax.axis_index("col")
    return r // 4, r % 4, c // 4, (c // 2) % 2, c % 2


def device(y, z, x, pair, core):
    return {"row": y * 4 + z, "col": x * 4 + pair * 2 + core}


def turn(v, by):
    return (v + by) % 4


class Post:
    def __init__(self, send_sem, recv_sem):
        self.send_sem = send_sem
        self.recv_sem = recv_sem
        self.sent = []

    def send(self, src, dst, peer):
        at = len(self.sent)
        copy = pltpu.make_async_remote_copy(
            src_ref=src,
            dst_ref=dst,
            send_sem=self.send_sem.at[at],
            recv_sem=self.recv_sem.at[at],
            device_id=peer,
            device_id_type=pl.DeviceIdType.MESH,
        )
        copy.start()
        self.sent.append(copy)
        return copy

    def finish(self):
        for copy in self.sent:
            copy.wait_send()


def count_of(condition):
    return jnp.where(condition, 1, 0).astype(I32)


def iota(shape, axis):
    return lax.broadcasted_iota(I32, shape, axis)


def stand(row):
    eye = iota((EDGE, EDGE), 0) == iota((EDGE, EDGE), 1)
    parts = []
    for t in range(row.shape[1] // EDGE):
        wide = jnp.broadcast_to(row[:, t * EDGE : (t + 1) * EDGE], (EDGE, EDGE))
        parts.append(jnp.sum(jnp.where(eye, wide, jnp.zeros_like(wide)), axis=1, keepdims=True))
    return jnp.concatenate(parts, axis=0)


def order_slots(col_row, row_row, lists, empty):
    slots, spots = col_row.shape[1], lists.shape[1]
    col, row = stand(col_row), stand(row_row)
    earlier = iota((slots, slots), 1) < iota((slots, slots), 0)
    equal = jnp.broadcast_to(col_row, (slots, slots)) == jnp.broadcast_to(col, (slots, slots))
    within = jnp.sum(count_of(equal & earlier), axis=1, keepdims=True)
    hit = jnp.broadcast_to(col, (slots, EDGE)) == iota((slots, EDGE), 1)
    pairs_row = (jnp.sum(count_of(hit), axis=0, keepdims=True) + 1) // 2
    pairs_row = jnp.where(iota((1, EDGE), 1) < TILES, pairs_row, 0)
    pairs_col = stand(pairs_row)
    square = (EDGE, EDGE)
    start_col = jnp.sum(
        jnp.where(iota(square, 1) < iota(square, 0), jnp.broadcast_to(pairs_row, square), 0),
        axis=1, keepdims=True,
    )
    start_row = jnp.sum(
        jnp.where(iota(square, 0) < iota(square, 1), jnp.broadcast_to(pairs_col, square), 0),
        axis=0, keepdims=True,
    )
    start = jnp.sum(
        jnp.where(hit, jnp.broadcast_to(start_row, (slots, EDGE)), 0), axis=1, keepdims=True
    )
    spot = jnp.where(col < TILES, 2 * start + within, -1)
    here = jnp.broadcast_to(spot, (slots, spots)) == iota((slots, spots), 1)
    lists[0:1, :] = empty + jnp.sum(
        jnp.where(here, iota((slots, spots), 0) - empty, 0), axis=0, keepdims=True
    )
    lists[1:2, :] = jnp.sum(
        jnp.where(here, jnp.broadcast_to(row, (slots, spots)), 0), axis=0, keepdims=True
    )
    begins = (jnp.broadcast_to(start_col, (EDGE, spots)) == iota((EDGE, spots), 1)) & (
        jnp.broadcast_to(pairs_col, (EDGE, spots)) > 0
    )
    lists[2:3, :] = 1 - jnp.sum(count_of(begins), axis=0, keepdims=True)
    last = jnp.where(pairs_row > 0, start_row + pairs_row - 1, PAIRS)
    lists[3:4, :] = jnp.concatenate([last, jnp.zeros((1, spots - EDGE), I32)], axis=1)
    lists[4:8, :] = jnp.zeros((4, spots), I32)


def layer_kernel(
    inputs_in, aggregated_in, grad_out_in, preact_in, inv_in, w_self_in, w_neigh_in,
    blocks_in, rows_in, cols_in, count_in, out, weights, bias, *scratch,
):
    (
        inputs, aggregated, grad_out, preact, w_self, w_neigh, masked_ref, self_term,
        blocks, prefix, partial, lists_v, lists,
        shares_y, from_y, shares_z, from_z, shares_x, from_x,
        work_a, from_core, work_b, from_pair, by_z, by_y, by_x,
        inv, block_rows, block_cols, block_count,
        send_sem, recv_sem, load_sem,
    ) = scratch[:33]
    flow_refs = [scratch[33 + i * 7 : 40 + i * 7] for i in range(HALVES * len(FLOWS))]
    strips = scratch[33 + 7 * HALVES * len(FLOWS) :]
    y, z, x, pair, core = place()
    rows, feat = inputs.shape
    cut = feat // HALVES
    right, left, opposite, other = turn(x, 1), turn(x, 3), turn(x, 2), 1 - pair
    to_pair = device(y, z, x, other, core)
    to_core = device(y, z, x, pair, 1 - core)
    peer_y = {by: device(turn(y, by), z, x, pair, core) for by in (1, 2, 3)}
    peer_z = {by: device(y, turn(z, by), x, pair, core) for by in (1, 2, 3)}
    peer_x = {by: device(y, z, turn(x, by), pair, core) for by in (1, 2, 3)}
    to_right, to_left = peer_x[1], peer_x[3]
    met = [to_pair, to_core] + [
        peer[by] for peer in (peer_y, peer_z, peer_x) for by in (1, 2, 3)
    ]
    barrier = pltpu.get_barrier_semaphore()
    for peer in met:
        pl.semaphore_signal(barrier, inc=1, device_id=peer, device_id_type=pl.DeviceIdType.MESH)
    post = Post(send_sem, recv_sem)
    peers = {"y": peer_y, "z": peer_z}
    own = {"y": y, "z": z}

    loads = []

    def load(src, dst):
        copy = pltpu.make_async_copy(src, dst, load_sem.at[len(loads)])
        copy.start()
        loads.append(copy)
        return copy

    half = rows // 2
    first = [load(w_neigh_in, w_neigh), load(inv_in, inv)]
    parts = []
    for h in range(2):
        span = pl.ds(h * half, half)
        parts.append(
            [load(preact_in.at[span], preact.at[span]), load(grad_out_in.at[span], grad_out.at[span])]
        )
    later = [load(w_self_in, w_self), load(inputs_in, inputs), load(aggregated_in, aggregated)]
    slots = blocks_in.shape[0]
    given = [
        load(rows_in, block_rows),
        load(cols_in, block_cols),
        load(count_in, block_count),
    ]
    fetched = load(blocks_in, blocks.at[pl.ds(0, slots)])

    per_shard = rows // EDGE

    def part(at_x, at_pair, at_core, h):
        shard = (at_x * 2 + at_pair) * 2 + at_core
        return pl.ds(shard * per_shard + h * (per_shard // 2), per_shard // 2)

    def gather(f):
        def send(where, peer):
            return post.send(strips[f].at[where], strips[f].at[where], peer)

        passed = []

        def arrived(copy, at_x, at_pair, h):
            copy.wait_recv()
            where = part(at_x, at_pair, core, h)
            passed.append(send(where, to_core))
            return where

        own_right, own_left, own_pair = {}, {}, {}
        for h in range(2):
            mine = part(x, pair, core, h)
            own_right[h] = send(mine, to_right)
            own_left[h] = send(mine, to_left)
            own_pair[h] = send(mine, to_pair)
            passed.append(send(mine, to_core))
            yield
        far_0 = send(arrived(own_right[0], left, pair, 0), to_right)
        arrived(own_left[0], right, pair, 0)
        yield
        where = arrived(own_pair[0], x, other, 0)
        other_right_0, other_left_0 = send(where, to_right), send(where, to_left)
        yield
        far_1 = send(arrived(own_left[1], right, pair, 1), to_left)
        arrived(own_right[1], left, pair, 1)
        yield
        where = arrived(own_pair[1], x, other, 1)
        other_right_1, other_left_1 = send(where, to_right), send(where, to_left)
        yield
        far_pair_0 = send(arrived(far_0, opposite, pair, 0), to_pair)
        far_pair_1 = send(arrived(far_1, opposite, pair, 1), to_pair)
        yield
        arrived(other_right_0, left, other, 0)
        arrived(other_left_0, right, other, 0)
        yield
        arrived(other_right_1, left, other, 1)
        arrived(other_left_1, right, other, 1)
        yield
        arrived(far_pair_0, opposite, other, 0)
        arrived(far_pair_1, opposite, other, 1)
        for copy in passed:
            copy.wait_recv()

    def product(f):
        for begin in range(0, PAIRS, PART):

            def body(u, total):
                for i in range(STRIDE):
                    at = begin + u * STRIDE + i
                    pick = (lists[0, 2 * at], lists[0, 2 * at + 1])
                    line = (lists[1, 2 * at], lists[1, 2 * at + 1])
                    go_on = lists[2, at] == 1
                    total = jnp.where(go_on, total, jnp.zeros_like(total)) + lax.dot_general(
                        jnp.concatenate([blocks[pick[0]], blocks[pick[1]]], axis=0),
                        jnp.concatenate([strips[f][line[0]], strips[f][line[1]]], axis=0),
                        (((0,), (0,)), ((), ())),
                        preferred_element_type=F32,
                    )
                    prefix[at] = total
                return total

            before = prefix[begin - 1] if begin else jnp.zeros((EDGE, cut), F32)
            lax.fori_loop(0, PART // STRIDE, body, before)
            yield

        def leave(g, carry):
            for i in range(4):
                at = g * 4 + i
                span = pl.ds(pl.multiple_of(at * EDGE, EDGE), EDGE)
                partial[f, span, :] = prefix[lists[3, at]].astype(BF16)
            return carry

        lax.fori_loop(0, TILES // 4, leave, 0)

    def flow(refs, f, first, second, offset, span):
        via_a, left_a, right_a, sum_a, hold, via_b, side_b = refs
        h = span // 2
        halves = (slice(0, h), slice(h, span))
        ahead_a, back_a = peers[first][1], peers[first][3]
        ahead_b, back_b = peers[second][1], peers[second][3]
        order = (2, 1, 3, 0)

        def piece(by_a, by_b, k):
            at = {first: turn(own[first], by_a), second: turn(own[second], by_b)}
            start = (at["y"] * 4 + at["z"]) * rows + offset
            if k is None:
                return pl.ds(pl.multiple_of(start, 128), span)
            return pl.ds(pl.multiple_of(start + k * h, 64), h)

        far, near = {}, {}

        def launch(i):
            b = order[i]
            far[i] = (
                post.send(partial.at[f, piece(2, b, 0)], via_a.at[i, 0], ahead_a),
                post.send(partial.at[f, piece(2, b, 1)], via_a.at[i, 1], back_a),
            )
            near[i] = [
                post.send(partial.at[f, piece(1, b, 1)], left_a.at[i, pl.ds(h, h)], ahead_a),
                post.send(partial.at[f, piece(3, b, 0)], right_a.at[i, pl.ds(0, h)], back_a),
            ]

        def relay(i):
            b = order[i]
            far[i][0].wait_recv()
            sum_a[i, 0] = (
                via_a[i, 0].astype(F32) + partial[f, piece(1, b, 0), :].astype(F32)
            ).astype(BF16)
            near[i].append(post.send(sum_a.at[i, 0], left_a.at[i, pl.ds(0, h)], ahead_a))
            far[i][1].wait_recv()
            sum_a[i, 1] = (
                via_a[i, 1].astype(F32) + partial[f, piece(3, b, 1), :].astype(F32)
            ).astype(BF16)
            near[i].append(post.send(sum_a.at[i, 1], right_a.at[i, pl.ds(h, h)], back_a))

        def close(i):
            for copy in near[i]:
                copy.wait_recv()
            return (
                partial[f, piece(0, order[i], None), :].astype(F32)
                + left_a[i].astype(F32)
                + right_a[i].astype(F32)
            )

        launch(0)
        launch(1)
        yield
        sent_b = []
        for i in range(5):
            if i < 4:
                relay(i)
                if i + 2 < 4:
                    launch(i + 2)
                yield
            if i == 0:
                continue
            done = close(i - 1)
            if i == 1:
                hold[0] = done.astype(BF16)
                far_b = (
                    post.send(hold.at[0, pl.ds(0, h)], via_b.at[0], ahead_b),
                    post.send(hold.at[0, pl.ds(h, h)], via_b.at[1], back_b),
                )
            elif i == 2:
                hold[1, pl.ds(h, h), :] = done[halves[1], :].astype(BF16)
                sent_b.append(
                    post.send(hold.at[1, pl.ds(h, h)], side_b.at[0, pl.ds(h, h)], ahead_b)
                )
                far_b[0].wait_recv()
                hold[1, pl.ds(0, h), :] = (done[halves[0], :] + via_b[0].astype(F32)).astype(BF16)
                sent_b.append(
                    post.send(hold.at[1, pl.ds(0, h)], side_b.at[0, pl.ds(0, h)], ahead_b)
                )
            elif i == 3:
                hold[2, pl.ds(0, h), :] = done[halves[0], :].astype(BF16)
                sent_b.append(
                    post.send(hold.at[2, pl.ds(0, h)], side_b.at[1, pl.ds(0, h)], back_b)
                )
                far_b[1].wait_recv()
                hold[2, pl.ds(h, h), :] = (done[halves[1], :] + via_b[1].astype(F32)).astype(BF16)
                sent_b.append(
                    post.send(hold.at[2, pl.ds(h, h)], side_b.at[1, pl.ds(h, h)], back_b)
                )
            else:
                done = done + self_term[pl.ds(offset, span), f * cut : (f + 1) * cut]
                yield
                for copy in sent_b:
                    copy.wait_recv()
                out[pl.ds(offset, span), f * cut : (f + 1) * cut] = (
                    done + side_b[0].astype(F32) + side_b[1].astype(F32)
                ).astype(BF16)
            yield

    def weight_sums():
        copies = [
            post.send(shares_y.at[turn(y, by)], from_y.at[y], peer_y[by]) for by in (1, 2, 3)
        ]
        from_y[y] = shares_y[y]
        yield
        for copy in copies:
            copy.wait_recv()
        total_y = from_y[0] + from_y[1] + from_y[2] + from_y[3]
        for q in range(4):
            shares_z[q, :small, :] = total_y[q * small : (q + 1) * small, :]
            shares_z[q, small:, :] = total_y[tall:, :]
        copies = [
            post.send(shares_z.at[turn(z, by)], from_z.at[z], peer_z[by]) for by in (1, 2, 3)
        ]
        from_z[z] = shares_z[z]
        yield
        for copy in copies:
            copy.wait_recv()
        total_z = from_z[0] + from_z[1] + from_z[2] + from_z[3]
        for q in range(4):
            shares_x[q, :PAD, :] = total_z[q * PAD : (q + 1) * PAD, :]
            shares_x[q, PAD:, :] = total_z[4 * PAD :, :]
        copies = [
            post.send(shares_x.at[turn(x, by)], from_x.at[x], peer_x[by]) for by in (1, 2, 3)
        ]
        from_x[x] = shares_x[x]
        yield
        for copy in copies:
            copy.wait_recv()
        work_a[...] = from_x[0] + from_x[1] + from_x[2] + from_x[3]
        copy = post.send(work_a, from_core, to_core)
        yield
        copy.wait_recv()
        work_b[...] = work_a[...] + from_core[...]
        copy = post.send(work_b, from_pair, to_pair)
        yield
        copy.wait_recv()
        done = work_b[...] + from_pair[...]
        bias[...] = done[PAD:, :]
        by_z[z] = done[:PAD, :]
        copies = [post.send(by_z.at[z], by_z.at[z], peer_z[by]) for by in (1, 2, 3)]
        yield
        for copy in copies:
            copy.wait_recv()
        by_y[y] = by_z[...]
        copies = [post.send(by_z, by_y.at[y], peer_y[by]) for by in (1, 2, 3)]
        yield
        for copy in copies:
            copy.wait_recv()
        by_x[x] = by_y[...]
        copies = [post.send(by_y, by_x.at[x], peer_x[by]) for by in (1, 2, 3)]
        yield
        yield
        for copy in copies:
            copy.wait_recv()
        for at_y in range(4):
            for at_z in range(4):
                for at_x in range(4):
                    first = ((at_y * 4 + at_z) * 4 + at_x) * PAD
                    weights[first : first + PAD, :] = by_x[at_x, at_y, at_z]

    def step(one, count=1):
        for unused in range(count):
            if next(one, "end") == "end":
                return False
        return True

    gathers = [gather(f) for f in range(HALVES)]
    for copy in first:
        copy.wait()
    scales = inv[...].astype(F32).reshape(rows // EDGE, EDGE)
    for h in range(2):
        for copy in parts[h]:
            copy.wait()
        base = h * half
        grads = grad_out[base : base + half, :]
        masked = jnp.where(preact[base : base + half, :] > 0, grads, jnp.zeros_like(grads))
        masked_ref[base : base + half, :] = masked
        projected = lax.dot_general(
            masked, w_neigh[...], (((1,), (1,)), ((), ())), preferred_element_type=F32
        )
        for t in range(half // EDGE):
            at = h * (half // EDGE) + t
            scaled = (projected[t * EDGE : (t + 1) * EDGE, :] * stand(scales[at : at + 1, :])).astype(BF16)
            mine = ((x * 2 + pair) * 2 + core) * per_shard + at
            for f in range(HALVES):
                strips[f][mine] = scaled[:, f * cut : (f + 1) * cut]
        if h == 0:
            pl.semaphore_wait(barrier, len(met))
        step(gathers[0])

    tall = 2 * feat // 4
    small = tall // 4
    for copy in later:
        copy.wait()
    masked = masked_ref[...]
    bias_part = jnp.sum(masked.astype(F32), axis=0, keepdims=True)
    for which, factor in enumerate((inputs, aggregated)):
        result = lax.dot_general(
            factor[...], masked, (((0,), (0,)), ((), ())), preferred_element_type=F32
        )
        for q in range(2):
            shares_y[which * 2 + q, :tall, :] = result[q * tall : (q + 1) * tall, :]
            shares_y[which * 2 + q, tall:, :] = jnp.broadcast_to(bias_part, (PAD, feat))
    sums = weight_sums()
    step(sums)
    step(gathers[0])
    blocks[slots] = jnp.zeros((EDGE, EDGE), BF16)
    prefix[PAIRS] = jnp.zeros((EDGE, cut), F32)
    for copy in given:
        copy.wait()
    spots = slots + -slots % EDGE
    spot = iota((1, spots), 1)

    def line_up(u, rows_of):
        col_row, row_row = rows_of
        for i in range(8):
            at = u * 8 + i
            col_row = jnp.where(spot == at, block_cols[at], col_row)
            row_row = jnp.where(spot == at, block_rows[at], row_row)
        return col_row, row_row

    blank = jnp.zeros((1, spots), I32)
    col_row, row_row = lax.fori_loop(0, slots // 8, line_up, (blank, blank))
    live = spot < block_count[0, 0]
    order_slots(jnp.where(live, col_row, EDGE - 1), row_row, lists_v, slots)
    listed = load(lists_v, lists)
    step(gathers[0])
    self_term[...] = lax.dot_general(
        masked, w_self[...], (((1,), (1,)), ((), ())), preferred_element_type=F32
    )
    listed.wait()
    fetched.wait()
    step(gathers[0], 2)
    for f in range(1, HALVES):
        step(gathers[f], 2)
    while step(gathers[0]):
        pass
    step(sums)

    flows = []
    for f in range(HALVES):
        work = product(f)
        busy = True
        while busy:
            busy = step(work)
            if f + 1 < HALVES:
                step(gathers[f + 1], 2)
            flows = [one for one in flows if step(one)]
            step(sums)
        if f + 1 < HALVES:
            while step(gathers[f + 1]):
                pass
        flows += [
            flow(flow_refs[f * len(FLOWS) + i], f, *spec) for i, spec in enumerate(FLOWS)
        ]
        flows = [one for one in flows if step(one)]
    while flows:
        flows = [one for one in flows if step(one)]
        step(sums)
    while step(sums):
        pass
    post.finish()


def local(
    inputs, aggregated, grad_out, preact, inv_degree, w_self, w_neigh,
    blocks, block_rows, block_cols, block_count,
):
    rows, feat = inputs.shape
    cut = feat // HALVES
    strip_rows = rows * lax.axis_size("col")
    group_rows = rows * lax.axis_size("row")
    vmem = pl.BlockSpec(memory_space=pltpu.VMEM)
    hbm = pl.BlockSpec(memory_space=pltpu.HBM)
    dma = pltpu.SemaphoreType.DMA
    slots = blocks.shape[0]
    tall = 2 * feat // 4
    small = tall // 4
    whole = pltpu.VMEM((rows, feat), BF16)
    square = pltpu.VMEM((feat, feat), BF16)
    two = (2 * PAD, feat)
    sends = HALVES * (30 + 30 * len(FLOWS)) + 20
    scratch = [
        whole, whole, whole, whole, square, square, whole, pltpu.VMEM((rows, feat), F32),
        pltpu.VMEM((slots + 1, EDGE, EDGE), BF16),
        pltpu.VMEM((PAIRS + 1, EDGE, cut), F32),
        pltpu.VMEM((HALVES, group_rows, cut), BF16),
        pltpu.VMEM((8, 512), I32),
        pltpu.SMEM((8, 512), I32),
        pltpu.VMEM((4, tall + PAD, feat), F32),
        pltpu.VMEM((4, tall + PAD, feat), F32),
        pltpu.VMEM((4, small + PAD, feat), F32),
        pltpu.VMEM((4, small + PAD, feat), F32),
        pltpu.VMEM((4,) + two, F32),
        pltpu.VMEM((4,) + two, F32),
        pltpu.VMEM(two, F32),
        pltpu.VMEM(two, F32),
        pltpu.VMEM(two, F32),
        pltpu.VMEM(two, F32),
        pltpu.VMEM((4, PAD, feat), F32),
        pltpu.VMEM((4, 4, PAD, feat), F32),
        pltpu.VMEM((4, 4, 4, PAD, feat), F32),
        pltpu.VMEM((rows,), BF16),
        pltpu.SMEM((slots,), I32),
        pltpu.SMEM((slots,), I32),
        pltpu.SMEM((1, 1), I32),
        dma((sends,)),
        dma((sends,)),
        dma((14,)),
    ]
    for unused in range(HALVES):
        for unused_a, unused_b, unused_c, span in FLOWS:
            scratch += [
                pltpu.VMEM((4, 2, span // 2, cut), BF16),
                pltpu.VMEM((4, span, cut), BF16),
                pltpu.VMEM((4, span, cut), BF16),
                pltpu.VMEM((4, 2, span // 2, cut), BF16),
                pltpu.VMEM((3, span, cut), BF16),
                pltpu.VMEM((2, span // 2, cut), BF16),
                pltpu.VMEM((2, span, cut), BF16),
            ]
    scratch += [pltpu.VMEM((strip_rows // EDGE, EDGE, cut), BF16)] * HALVES
    grad_inputs, weights, bias = pl.pallas_call(
        layer_kernel,
        out_shape=(
            jax.ShapeDtypeStruct((rows, feat), BF16),
            jax.ShapeDtypeStruct((2 * feat, feat), F32),
            jax.ShapeDtypeStruct((PAD, feat), F32),
        ),
        in_specs=[hbm] * 11,
        out_specs=(vmem, vmem, vmem),
        scratch_shapes=scratch,
        compiler_params=pltpu.CompilerParams(
            collective_id=0, has_side_effects=True, vmem_limit_bytes=LIMIT * 2**20
        ),
        name="layer",
    )(
        inputs, aggregated, grad_out, preact, inv_degree, w_self, w_neigh,
        blocks, block_rows, block_cols, block_count,
    )
    return grad_inputs, weights[:feat], weights[feat:], bias[0]


def solution(mesh):
    both = ("row", "col")
    return jax.shard_map(
        local,
        mesh=mesh,
        in_specs=(
            P(both, None), P(both, None), P(both, None), P(both, None), P(both),
            P(), P(),
            P(both, None, None), P(both), P(both), P("row", "col"),
        ),
        out_specs=(P(both, None), P(), P(), P()),
        check_vma=False,
    )
```

```python
import functools

import jax
import jax.numpy as jnp
from jax import lax
from jax.experimental import pallas as pl
from jax.experimental.pallas import tpu as pltpu
from jax.sharding import PartitionSpec as P

EDGE = 128
HALVES = 2
TILES = 64
I32 = jnp.int32
F32 = jnp.float32
BF16 = jnp.bfloat16
FLOWS = (("y", "z", 0, 384), ("z", "y", 384, 128))
PAD = 8
LIMIT = 62
SUM_TURNS = (3, 6, 8, 10, 12, 15, 18, 21)
PAIRS = 200
STRIDE = 20
PART = 40


def place():
    r = lax.axis_index("row")
    c = lax.axis_index("col")
    return r // 4, r % 4, c // 4, (c // 2) % 2, c % 2


def device(y, z, x, pair, core):
    return {"row": y * 4 + z, "col": x * 4 + pair * 2 + core}


def turn(v, by):
    return (v + by) % 4


class Post:
    def __init__(self, send_sem, recv_sem):
        self.send_sem = send_sem
        self.recv_sem = recv_sem
        self.sent = []

    def send(self, src, dst, peer):
        at = len(self.sent)
        copy = pltpu.make_async_remote_copy(
            src_ref=src,
            dst_ref=dst,
            send_sem=self.send_sem.at[at],
            recv_sem=self.recv_sem.at[at],
            device_id=peer,
            device_id_type=pl.DeviceIdType.MESH,
        )
        copy.start()
        self.sent.append(copy)
        return copy

    def finish(self):
        for copy in self.sent:
            copy.wait_send()


def count_of(condition):
    return jnp.where(condition, 1, 0).astype(I32)


def iota(shape, axis):
    return lax.broadcasted_iota(I32, shape, axis)


def stand(row):
    eye = iota((EDGE, EDGE), 0) == iota((EDGE, EDGE), 1)
    parts = []
    for t in range(row.shape[1] // EDGE):
        wide = jnp.broadcast_to(row[:, t * EDGE : (t + 1) * EDGE], (EDGE, EDGE))
        parts.append(jnp.sum(jnp.where(eye, wide, jnp.zeros_like(wide)), axis=1, keepdims=True))
    return jnp.concatenate(parts, axis=0)


def order_slots(col_row, row_row, lists, empty):
    slots, spots = col_row.shape[1], lists.shape[1]
    col, row = stand(col_row), stand(row_row)
    earlier = iota((slots, slots), 1) < iota((slots, slots), 0)
    equal = jnp.broadcast_to(col_row, (slots, slots)) == jnp.broadcast_to(col, (slots, slots))
    within = jnp.sum(count_of(equal & earlier), axis=1, keepdims=True)
    hit = jnp.broadcast_to(col, (slots, EDGE)) == iota((slots, EDGE), 1)
    pairs_row = (jnp.sum(count_of(hit), axis=0, keepdims=True) + 1) // 2
    pairs_row = jnp.where(iota((1, EDGE), 1) < TILES, pairs_row, 0)
    pairs_col = stand(pairs_row)
    square = (EDGE, EDGE)
    start_col = jnp.sum(
        jnp.where(iota(square, 1) < iota(square, 0), jnp.broadcast_to(pairs_row, square), 0),
        axis=1, keepdims=True,
    )
    start_row = jnp.sum(
        jnp.where(iota(square, 0) < iota(square, 1), jnp.broadcast_to(pairs_col, square), 0),
        axis=0, keepdims=True,
    )
    start = jnp.sum(
        jnp.where(hit, jnp.broadcast_to(start_row, (slots, EDGE)), 0), axis=1, keepdims=True
    )
    spot = jnp.where(col < TILES, 2 * start + within, -1)
    here = jnp.broadcast_to(spot, (slots, spots)) == iota((slots, spots), 1)
    lists[0:1, :] = empty + jnp.sum(
        jnp.where(here, iota((slots, spots), 0) - empty, 0), axis=0, keepdims=True
    )
    lists[1:2, :] = jnp.sum(
        jnp.where(here, jnp.broadcast_to(row, (slots, spots)), 0), axis=0, keepdims=True
    )
    begins = (jnp.broadcast_to(start_col, (EDGE, spots)) == iota((EDGE, spots), 1)) & (
        jnp.broadcast_to(pairs_col, (EDGE, spots)) > 0
    )
    lists[2:3, :] = 1 - jnp.sum(count_of(begins), axis=0, keepdims=True)
    last = jnp.where(pairs_row > 0, start_row + pairs_row - 1, PAIRS)
    lists[3:4, :] = jnp.concatenate([last, jnp.zeros((1, spots - EDGE), I32)], axis=1)
    lists[4:8, :] = jnp.zeros((4, spots), I32)


def layer_kernel(
    inputs_in, aggregated_in, grad_out_in, preact_in, inv_in, w_self_in, w_neigh_in,
    blocks_in, rows_in, cols_in, count_in, out_hbm, weights_hbm, bias_hbm, *scratch,
):
    (
        inputs, aggregated, grad_out, preact, w_self, w_neigh, masked_ref, self_term,
        blocks, prefix, partial, lists_v, lists,
        shares_y, from_y, shares_z, from_z, shares_x, from_x,
        work_a, from_core, work_b, from_pair, by_z, by_y, by_x,
        inv, block_rows, block_cols, block_count, out, weights, bias,
        send_sem, recv_sem, load_sem,
    ) = scratch[:36]
    flow_refs = [scratch[36 + i * 7 : 43 + i * 7] for i in range(HALVES * len(FLOWS))]
    strips = scratch[36 + 7 * HALVES * len(FLOWS) :]
    y, z, x, pair, core = place()
    rows, feat = inputs.shape
    cut = feat // HALVES
    right, left, opposite, other = turn(x, 1), turn(x, 3), turn(x, 2), 1 - pair
    to_pair = device(y, z, x, other, core)
    to_core = device(y, z, x, pair, 1 - core)
    peer_y = {by: device(turn(y, by), z, x, pair, core) for by in (1, 2, 3)}
    peer_z = {by: device(y, turn(z, by), x, pair, core) for by in (1, 2, 3)}
    peer_x = {by: device(y, z, turn(x, by), pair, core) for by in (1, 2, 3)}
    to_right, to_left = peer_x[1], peer_x[3]
    met = [to_pair, to_core] + [
        peer[by] for peer in (peer_y, peer_z, peer_x) for by in (1, 2, 3)
    ]
    barrier = pltpu.get_barrier_semaphore()
    for peer in met:
        pl.semaphore_signal(barrier, inc=1, device_id=peer, device_id_type=pl.DeviceIdType.MESH)
    post = Post(send_sem, recv_sem)
    peers = {"y": peer_y, "z": peer_z}
    own = {"y": y, "z": z}

    loads = []

    def load(src, dst):
        copy = pltpu.make_async_copy(src, dst, load_sem.at[len(loads)])
        copy.start()
        loads.append(copy)
        return copy

    half = rows // 2
    first = [load(w_neigh_in, w_neigh), load(inv_in, inv)]
    parts = []
    for h in range(2):
        span = pl.ds(h * half, half)
        parts.append(
            [load(preact_in.at[span], preact.at[span]), load(grad_out_in.at[span], grad_out.at[span])]
        )
    later = [load(w_self_in, w_self), load(inputs_in, inputs), load(aggregated_in, aggregated)]
    slots = blocks_in.shape[0]
    given = [
        load(rows_in, block_rows),
        load(cols_in, block_cols),
        load(count_in, block_count),
    ]
    fetched = load(blocks_in, blocks.at[pl.ds(0, slots)])

    per_shard = rows // EDGE

    def part(at_x, at_pair, at_core, h):
        shard = (at_x * 2 + at_pair) * 2 + at_core
        return pl.ds(shard * per_shard + h * (per_shard // 2), per_shard // 2)

    def gather(f):
        def send(where, peer):
            return post.send(strips[f].at[where], strips[f].at[where], peer)

        passed = []

        def arrived(copy, at_x, at_pair, h):
            copy.wait_recv()
            where = part(at_x, at_pair, core, h)
            passed.append(send(where, to_core))
            return where

        own_right, own_left, own_pair = {}, {}, {}
        for h in range(2):
            mine = part(x, pair, core, h)
            own_right[h] = send(mine, to_right)
            own_left[h] = send(mine, to_left)
            own_pair[h] = send(mine, to_pair)
            passed.append(send(mine, to_core))
            yield
        far_0 = send(arrived(own_right[0], left, pair, 0), to_right)
        arrived(own_left[0], right, pair, 0)
        yield
        where = arrived(own_pair[0], x, other, 0)
        other_right_0, other_left_0 = send(where, to_right), send(where, to_left)
        yield
        far_1 = send(arrived(own_left[1], right, pair, 1), to_left)
        arrived(own_right[1], left, pair, 1)
        yield
        where = arrived(own_pair[1], x, other, 1)
        other_right_1, other_left_1 = send(where, to_right), send(where, to_left)
        yield
        far_pair_0 = send(arrived(far_0, opposite, pair, 0), to_pair)
        far_pair_1 = send(arrived(far_1, opposite, pair, 1), to_pair)
        yield
        arrived(other_right_0, left, other, 0)
        arrived(other_left_0, right, other, 0)
        yield
        arrived(other_right_1, left, other, 1)
        arrived(other_left_1, right, other, 1)
        yield
        arrived(far_pair_0, opposite, other, 0)
        arrived(far_pair_1, opposite, other, 1)
        for copy in passed:
            copy.wait_recv()

    def product(f):
        for begin in range(0, PAIRS, PART):

            def body(u, total):
                for i in range(STRIDE):
                    at = begin + u * STRIDE + i
                    pick = (lists[0, 2 * at], lists[0, 2 * at + 1])
                    line = (lists[1, 2 * at], lists[1, 2 * at + 1])
                    go_on = lists[2, at] == 1
                    total = jnp.where(go_on, total, jnp.zeros_like(total)) + lax.dot_general(
                        jnp.concatenate([blocks[pick[0]], blocks[pick[1]]], axis=0),
                        jnp.concatenate([strips[f][line[0]], strips[f][line[1]]], axis=0),
                        (((0,), (0,)), ((), ())),
                        preferred_element_type=F32,
                    )
                    prefix[at] = total
                return total

            before = prefix[begin - 1] if begin else jnp.zeros((EDGE, cut), F32)
            lax.fori_loop(0, PART // STRIDE, body, before)
            yield

        def leave(g, carry):
            for i in range(4):
                at = g * 4 + i
                span = pl.ds(pl.multiple_of(at * EDGE, EDGE), EDGE)
                partial[f, span, :] = prefix[lists[3, at]].astype(BF16)
            return carry

        lax.fori_loop(0, TILES // 4, leave, 0)

    def flow(refs, f, first, second, offset, span):
        via_a, left_a, right_a, sum_a, hold, via_b, side_b = refs
        h = span // 2
        halves = (slice(0, h), slice(h, span))
        ahead_a, back_a = peers[first][1], peers[first][3]
        ahead_b, back_b = peers[second][1], peers[second][3]
        order = (2, 1, 3, 0)

        def piece(by_a, by_b, k):
            at = {first: turn(own[first], by_a), second: turn(own[second], by_b)}
            start = (at["y"] * 4 + at["z"]) * rows + offset
            if k is None:
                return pl.ds(pl.multiple_of(start, 128), span)
            return pl.ds(pl.multiple_of(start + k * h, 64), h)

        far, near = {}, {}

        def launch(i):
            b = order[i]
            far[i] = (
                post.send(partial.at[f, piece(2, b, 0)], via_a.at[i, 0], ahead_a),
                post.send(partial.at[f, piece(2, b, 1)], via_a.at[i, 1], back_a),
            )
            near[i] = [
                post.send(partial.at[f, piece(1, b, 1)], left_a.at[i, pl.ds(h, h)], ahead_a),
                post.send(partial.at[f, piece(3, b, 0)], right_a.at[i, pl.ds(0, h)], back_a),
            ]

        def relay(i):
            b = order[i]
            far[i][0].wait_recv()
            sum_a[i, 0] = (
                via_a[i, 0].astype(F32) + partial[f, piece(1, b, 0), :].astype(F32)
            ).astype(BF16)
            near[i].append(post.send(sum_a.at[i, 0], left_a.at[i, pl.ds(0, h)], ahead_a))
            far[i][1].wait_recv()
            sum_a[i, 1] = (
                via_a[i, 1].astype(F32) + partial[f, piece(3, b, 1), :].astype(F32)
            ).astype(BF16)
            near[i].append(post.send(sum_a.at[i, 1], right_a.at[i, pl.ds(h, h)], back_a))

        def close(i):
            for copy in near[i]:
                copy.wait_recv()
            return (
                partial[f, piece(0, order[i], None), :].astype(F32)
                + left_a[i].astype(F32)
                + right_a[i].astype(F32)
            )

        launch(0)
        launch(1)
        yield
        sent_b = []
        for i in range(5):
            if i < 4:
                relay(i)
                if i + 2 < 4:
                    launch(i + 2)
                yield
            if i == 0:
                continue
            done = close(i - 1)
            if i == 1:
                hold[0] = done.astype(BF16)
                far_b = (
                    post.send(hold.at[0, pl.ds(0, h)], via_b.at[0], ahead_b),
                    post.send(hold.at[0, pl.ds(h, h)], via_b.at[1], back_b),
                )
            elif i == 2:
                hold[1, pl.ds(h, h), :] = done[halves[1], :].astype(BF16)
                sent_b.append(
                    post.send(hold.at[1, pl.ds(h, h)], side_b.at[0, pl.ds(h, h)], ahead_b)
                )
                far_b[0].wait_recv()
                hold[1, pl.ds(0, h), :] = (done[halves[0], :] + via_b[0].astype(F32)).astype(BF16)
                sent_b.append(
                    post.send(hold.at[1, pl.ds(0, h)], side_b.at[0, pl.ds(0, h)], ahead_b)
                )
            elif i == 3:
                hold[2, pl.ds(0, h), :] = done[halves[0], :].astype(BF16)
                sent_b.append(
                    post.send(hold.at[2, pl.ds(0, h)], side_b.at[1, pl.ds(0, h)], back_b)
                )
                far_b[1].wait_recv()
                hold[2, pl.ds(h, h), :] = (done[halves[1], :] + via_b[1].astype(F32)).astype(BF16)
                sent_b.append(
                    post.send(hold.at[2, pl.ds(h, h)], side_b.at[1, pl.ds(h, h)], back_b)
                )
            else:
                done = done + self_term[pl.ds(offset, span), f * cut : (f + 1) * cut]
                yield
                for copy in sent_b:
                    copy.wait_recv()
                out[pl.ds(offset, span), f * cut : (f + 1) * cut] = (
                    done + side_b[0].astype(F32) + side_b[1].astype(F32)
                ).astype(BF16)
            yield

    def weight_sums():
        copies = [
            post.send(shares_y.at[turn(y, by)], from_y.at[y], peer_y[by]) for by in (1, 2, 3)
        ]
        from_y[y] = shares_y[y]
        yield
        for copy in copies:
            copy.wait_recv()
        total_y = from_y[0] + from_y[1] + from_y[2] + from_y[3]
        for q in range(4):
            shares_z[q, :small, :] = total_y[q * small : (q + 1) * small, :]
            shares_z[q, small:, :] = total_y[tall:, :]
        copies = [
            post.send(shares_z.at[turn(z, by)], from_z.at[z], peer_z[by]) for by in (1, 2, 3)
        ]
        from_z[z] = shares_z[z]
        yield
        for copy in copies:
            copy.wait_recv()
        total_z = from_z[0] + from_z[1] + from_z[2] + from_z[3]
        for q in range(4):
            shares_x[q, :PAD, :] = total_z[q * PAD : (q + 1) * PAD, :]
            shares_x[q, PAD:, :] = total_z[4 * PAD :, :]
        copies = [
            post.send(shares_x.at[turn(x, by)], from_x.at[x], peer_x[by]) for by in (1, 2, 3)
        ]
        from_x[x] = shares_x[x]
        yield
        for copy in copies:
            copy.wait_recv()
        work_a[...] = from_x[0] + from_x[1] + from_x[2] + from_x[3]
        copy = post.send(work_a, from_core, to_core)
        yield
        copy.wait_recv()
        work_b[...] = work_a[...] + from_core[...]
        copy = post.send(work_b, from_pair, to_pair)
        yield
        copy.wait_recv()
        done = work_b[...] + from_pair[...]
        bias[...] = done[PAD:, :]
        by_z[z] = done[:PAD, :]
        copies = [post.send(by_z.at[z], by_z.at[z], peer_z[by]) for by in (1, 2, 3)]
        yield
        for copy in copies:
            copy.wait_recv()
        by_y[y] = by_z[...]
        copies = [post.send(by_z, by_y.at[y], peer_y[by]) for by in (1, 2, 3)]
        yield
        for copy in copies:
            copy.wait_recv()
        by_x[x] = by_y[...]
        copies = [post.send(by_y, by_x.at[x], peer_x[by]) for by in (1, 2, 3)]
        yield
        for copy in copies:
            copy.wait_recv()
        for at_y in range(4):
            for at_z in range(4):
                for at_x in range(4):
                    first = ((at_y * 4 + at_z) * 4 + at_x) * PAD
                    weights[first : first + PAD, :] = by_x[at_x, at_y, at_z]

    def step(one, count=1):
        for unused in range(count):
            if next(one, "end") == "end":
                return False
        return True

    gathers = [gather(f) for f in range(HALVES)]
    for copy in first:
        copy.wait()
    scales = inv[...].astype(F32).reshape(rows // EDGE, EDGE)
    for h in range(2):
        for copy in parts[h]:
            copy.wait()
        base = h * half
        grads = grad_out[base : base + half, :]
        masked = jnp.where(preact[base : base + half, :] > 0, grads, jnp.zeros_like(grads))
        masked_ref[base : base + half, :] = masked
        projected = lax.dot_general(
            masked, w_neigh[...], (((1,), (1,)), ((), ())), preferred_element_type=F32
        )
        for t in range(half // EDGE):
            at = h * (half // EDGE) + t
            scaled = (projected[t * EDGE : (t + 1) * EDGE, :] * stand(scales[at : at + 1, :])).astype(BF16)
            mine = ((x * 2 + pair) * 2 + core) * per_shard + at
            for f in range(HALVES):
                strips[f][mine] = scaled[:, f * cut : (f + 1) * cut]
        if h == 0:
            pl.semaphore_wait(barrier, len(met))
        step(gathers[0])
    for f in range(1, HALVES):
        step(gathers[f], 2)

    tall = 2 * feat // 4
    small = tall // 4

    def sort_chore():
        blocks[slots] = jnp.zeros((EDGE, EDGE), BF16)
        prefix[PAIRS] = jnp.zeros((EDGE, cut), F32)
        for copy in given:
            copy.wait()
        spots = slots + -slots % EDGE
        spot = iota((1, spots), 1)

        def line_up(u, rows_of):
            col_row, row_row = rows_of
            for i in range(8):
                at = u * 8 + i
                col_row = jnp.where(spot == at, block_cols[at], col_row)
                row_row = jnp.where(spot == at, block_rows[at], row_row)
            return col_row, row_row

        blank = jnp.zeros((1, spots), I32)
        col_row, row_row = lax.fori_loop(0, slots // 8, line_up, (blank, blank))
        live = spot < block_count[0, 0]
        order_slots(jnp.where(live, col_row, EDGE - 1), row_row, lists_v, slots)
        return load(lists_v, lists)

    def weight_chore(which, factor):
        result = lax.dot_general(
            factor[...], masked_ref[...], (((0,), (0,)), ((), ())), preferred_element_type=F32
        )
        for q in range(2):
            shares_y[which * 2 + q, :tall, :] = result[q * tall : (q + 1) * tall, :]

    def bias_chore():
        bias_part = jnp.sum(masked_ref[...].astype(F32), axis=0, keepdims=True)
        for q in range(4):
            shares_y[q, tall:, :] = jnp.broadcast_to(bias_part, (PAD, feat))

    sums = weight_sums()
    listed = sort_chore()
    step(gathers[0], 2)
    later[0].wait()
    self_term[...] = lax.dot_general(
        masked_ref[...], w_self[...], (((1,), (1,)), ((), ())), preferred_element_type=F32
    )
    step(gathers[0], 2)
    later[1].wait()
    weight_chore(0, inputs)
    step(gathers[0])
    step(gathers[1])
    later[2].wait()
    weight_chore(1, aggregated)
    step(gathers[1])
    bias_chore()
    step(sums)
    step(gathers[0])
    step(gathers[1])
    step(gathers[0])
    step(gathers[1])
    step(gathers[0])
    listed.wait()
    fetched.wait()

    flows = []
    turns = 0
    for f in range(HALVES):
        work = product(f)
        busy = True
        while busy:
            busy = step(work)
            if f + 1 < HALVES:
                step(gathers[f + 1])
            flows = [one for one in flows if step(one)]
            turns += 1
            if turns in SUM_TURNS:
                step(sums)
        if f + 1 < HALVES:
            while step(gathers[f + 1]):
                pass
        flows += [
            flow(flow_refs[f * len(FLOWS) + i], f, *spec) for i, spec in enumerate(FLOWS)
        ]
        flows = [one for one in flows if step(one)]
    while flows:
        flows = [one for one in flows if step(one)]
        turns += 1
        if turns in SUM_TURNS:
            step(sums)
    while step(sums):
        pass
    results = [
        load(out, out_hbm), load(weights, weights_hbm), load(bias, bias_hbm)
    ]
    post.finish()
    for copy in results:
        copy.wait()


def leave_kernel(
    grads, weights, bias, grads_out, self_out, neigh_out, bias_out,
    grads_v, self_v, neigh_v, bias_v, sem_in, sem_out,
):
    feat = weights.shape[1]
    moves = (
        (weights.at[pl.ds(0, feat)], self_v, self_v, self_out),
        (weights.at[pl.ds(feat, feat)], neigh_v, neigh_v, neigh_out),
        (grads, grads_v, grads_v, grads_out),
        (bias, bias_v, bias_v.at[pl.ds(0, 1)], bias_out),
    )
    come = [pltpu.make_async_copy(m[0], m[1], sem_in.at[i]) for i, m in enumerate(moves)]
    go = [pltpu.make_async_copy(m[2], m[3], sem_out.at[i]) for i, m in enumerate(moves)]
    for copy in come:
        copy.start()
    for arrival, departure in zip(come, go):
        arrival.wait()
        departure.start()
    for copy in go:
        copy.wait()


def local(
    inputs, aggregated, grad_out, preact, inv_degree, w_self, w_neigh,
    blocks, block_rows, block_cols, block_count,
):
    rows, feat = inputs.shape
    cut = feat // HALVES
    strip_rows = rows * lax.axis_size("col")
    group_rows = rows * lax.axis_size("row")
    hbm = pl.BlockSpec(memory_space=pltpu.HBM)
    dma = pltpu.SemaphoreType.DMA
    slots = blocks.shape[0]
    tall = 2 * feat // 4
    small = tall // 4
    whole = pltpu.VMEM((rows, feat), BF16)
    square = pltpu.VMEM((feat, feat), BF16)
    two = (2 * PAD, feat)
    sends = HALVES * (30 + 30 * len(FLOWS)) + 20
    scratch = [
        whole, whole, whole, whole, square, square, whole, pltpu.VMEM((rows, feat), F32),
        pltpu.VMEM((slots + 1, EDGE, EDGE), BF16),
        pltpu.VMEM((PAIRS + 1, EDGE, cut), F32),
        pltpu.VMEM((HALVES, group_rows, cut), BF16),
        pltpu.VMEM((8, 512), I32),
        pltpu.SMEM((8, 512), I32),
        pltpu.VMEM((4, tall + PAD, feat), F32),
        pltpu.VMEM((4, tall + PAD, feat), F32),
        pltpu.VMEM((4, small + PAD, feat), F32),
        pltpu.VMEM((4, small + PAD, feat), F32),
        pltpu.VMEM((4,) + two, F32),
        pltpu.VMEM((4,) + two, F32),
        pltpu.VMEM(two, F32),
        pltpu.VMEM(two, F32),
        pltpu.VMEM(two, F32),
        pltpu.VMEM(two, F32),
        pltpu.VMEM((4, PAD, feat), F32),
        pltpu.VMEM((4, 4, PAD, feat), F32),
        pltpu.VMEM((4, 4, 4, PAD, feat), F32),
        pltpu.VMEM((rows,), BF16),
        pltpu.SMEM((slots,), I32),
        pltpu.SMEM((slots,), I32),
        pltpu.SMEM((1, 1), I32),
        whole,
        pltpu.VMEM((2 * feat, feat), F32),
        pltpu.VMEM((PAD, feat), F32),
        dma((sends,)),
        dma((sends,)),
        dma((20,)),
    ]
    for unused in range(HALVES):
        for unused_a, unused_b, unused_c, span in FLOWS:
            scratch += [
                pltpu.VMEM((4, 2, span // 2, cut), BF16),
                pltpu.VMEM((4, span, cut), BF16),
                pltpu.VMEM((4, span, cut), BF16),
                pltpu.VMEM((4, 2, span // 2, cut), BF16),
                pltpu.VMEM((3, span, cut), BF16),
                pltpu.VMEM((2, span // 2, cut), BF16),
                pltpu.VMEM((2, span, cut), BF16),
            ]
    scratch += [pltpu.VMEM((strip_rows // EDGE, EDGE, cut), BF16)] * HALVES
    results = pl.pallas_call(
        layer_kernel,
        out_shape=(
            jax.ShapeDtypeStruct((rows, feat), BF16),
            jax.ShapeDtypeStruct((2 * feat, feat), F32),
            jax.ShapeDtypeStruct((PAD, feat), F32),
        ),
        in_specs=[hbm] * 11,
        out_specs=(hbm, hbm, hbm),
        scratch_shapes=scratch,
        compiler_params=pltpu.CompilerParams(
            collective_id=0, has_side_effects=True, vmem_limit_bytes=LIMIT * 2**20
        ),
        name="layer",
    )(
        inputs, aggregated, grad_out, preact, inv_degree, w_self, w_neigh,
        blocks, block_rows, block_cols, block_count,
    )
    square_out = pltpu.VMEM((feat, feat), F32)
    grad_inputs, grad_self, grad_neigh, grad_bias = pl.pallas_call(
        leave_kernel,
        out_shape=(
            jax.ShapeDtypeStruct((rows, feat), BF16),
            jax.ShapeDtypeStruct((feat, feat), F32),
            jax.ShapeDtypeStruct((feat, feat), F32),
            jax.ShapeDtypeStruct((1, feat), F32),
        ),
        in_specs=[hbm] * 3,
        out_specs=[hbm] * 4,
        scratch_shapes=[
            whole, square_out, square_out, pltpu.VMEM((PAD, feat), F32), dma((4,)), dma((4,)),
        ],
        compiler_params=pltpu.CompilerParams(vmem_limit_bytes=LIMIT * 2**20),
        name="leave",
    )(*results)
    return grad_inputs, grad_self, grad_neigh, grad_bias.reshape(feat)


def solution(mesh):
    both = ("row", "col")
    return jax.shard_map(
        local,
        mesh=mesh,
        in_specs=(
            P(both, None), P(both, None), P(both, None), P(both, None), P(both),
            P(), P(),
            P(both, None, None), P(both), P(both), P("row", "col"),
        ),
        out_specs=(P(both, None), P(), P(), P()),
        check_vma=False,
    )
```

```python
import functools

import jax
import jax.numpy as jnp
from jax import lax
from jax.experimental import pallas as pl
from jax.experimental.pallas import tpu as pltpu
from jax.sharding import PartitionSpec as P

EDGE = 128
HALVES = 2
TILES = 64
I32 = jnp.int32
F32 = jnp.float32
BF16 = jnp.bfloat16
FLOWS = (("y", "z", 0, 384), ("z", "y", 384, 128))
PAD = 8
LIMIT = 62
SUM_TURNS = (3, 6, 8, 10, 12, 15, 18, 21)
PAIRS = 200
STRIDE = 20
PART = 40


def place():
    r = lax.axis_index("row")
    c = lax.axis_index("col")
    return r // 4, r % 4, c // 4, (c // 2) % 2, c % 2


def device(y, z, x, pair, core):
    return {"row": y * 4 + z, "col": x * 4 + pair * 2 + core}


def turn(v, by):
    return (v + by) % 4


class Post:
    def __init__(self, send_sem, recv_sem):
        self.send_sem = send_sem
        self.recv_sem = recv_sem
        self.sent = []

    def send(self, src, dst, peer):
        at = len(self.sent)
        copy = pltpu.make_async_remote_copy(
            src_ref=src,
            dst_ref=dst,
            send_sem=self.send_sem.at[at],
            recv_sem=self.recv_sem.at[at],
            device_id=peer,
            device_id_type=pl.DeviceIdType.MESH,
        )
        copy.start()
        self.sent.append(copy)
        return copy

    def finish(self):
        for copy in self.sent:
            copy.wait_send()


def count_of(condition):
    return jnp.where(condition, 1, 0).astype(I32)


def iota(shape, axis):
    return lax.broadcasted_iota(I32, shape, axis)


def stand(row):
    eye = iota((EDGE, EDGE), 0) == iota((EDGE, EDGE), 1)
    parts = []
    for t in range(row.shape[1] // EDGE):
        wide = jnp.broadcast_to(row[:, t * EDGE : (t + 1) * EDGE], (EDGE, EDGE))
        parts.append(jnp.sum(jnp.where(eye, wide, jnp.zeros_like(wide)), axis=1, keepdims=True))
    return jnp.concatenate(parts, axis=0)


def order_slots(col_row, row_row, lists, empty):
    slots, spots = col_row.shape[1], lists.shape[1]
    col, row = stand(col_row), stand(row_row)
    earlier = iota((slots, slots), 1) < iota((slots, slots), 0)
    equal = jnp.broadcast_to(col_row, (slots, slots)) == jnp.broadcast_to(col, (slots, slots))
    within = jnp.sum(count_of(equal & earlier), axis=1, keepdims=True)
    hit = jnp.broadcast_to(col, (slots, EDGE)) == iota((slots, EDGE), 1)
    pairs_row = (jnp.sum(count_of(hit), axis=0, keepdims=True) + 1) // 2
    pairs_row = jnp.where(iota((1, EDGE), 1) < TILES, pairs_row, 0)
    pairs_col = stand(pairs_row)
    square = (EDGE, EDGE)
    start_col = jnp.sum(
        jnp.where(iota(square, 1) < iota(square, 0), jnp.broadcast_to(pairs_row, square), 0),
        axis=1, keepdims=True,
    )
    start_row = jnp.sum(
        jnp.where(iota(square, 0) < iota(square, 1), jnp.broadcast_to(pairs_col, square), 0),
        axis=0, keepdims=True,
    )
    start = jnp.sum(
        jnp.where(hit, jnp.broadcast_to(start_row, (slots, EDGE)), 0), axis=1, keepdims=True
    )
    spot = jnp.where(col < TILES, 2 * start + within, -1)
    here = jnp.broadcast_to(spot, (slots, spots)) == iota((slots, spots), 1)
    lists[0:1, :] = empty + jnp.sum(
        jnp.where(here, iota((slots, spots), 0) - empty, 0), axis=0, keepdims=True
    )
    lists[1:2, :] = jnp.sum(
        jnp.where(here, jnp.broadcast_to(row, (slots, spots)), 0), axis=0, keepdims=True
    )
    begins = (jnp.broadcast_to(start_col, (EDGE, spots)) == iota((EDGE, spots), 1)) & (
        jnp.broadcast_to(pairs_col, (EDGE, spots)) > 0
    )
    lists[2:3, :] = 1 - jnp.sum(count_of(begins), axis=0, keepdims=True)
    last = jnp.where(pairs_row > 0, start_row + pairs_row - 1, PAIRS)
    lists[3:4, :] = jnp.concatenate([last, jnp.zeros((1, spots - EDGE), I32)], axis=1)
    lists[4:8, :] = jnp.zeros((4, spots), I32)


def layer_kernel(
    inputs_in, aggregated_in, grad_out_in, preact_in, inv_in, w_self_in, w_neigh_in,
    blocks_in, rows_in, cols_in, count_in, out_hbm, weights_hbm, bias_hbm, *scratch,
):
    (
        inputs, aggregated, grad_out, preact, w_self, w_neigh, masked_ref, self_term,
        blocks, prefix, partial, lists_v, lists,
        shares_y, from_y, shares_z, from_z, shares_x, from_x,
        work_a, from_core, work_b, from_pair, by_z, by_y, by_x,
        inv, block_rows, block_cols, block_count, out, weights, bias,
        send_sem, recv_sem, load_sem,
    ) = scratch[:36]
    flow_refs = [scratch[36 + i * 7 : 43 + i * 7] for i in range(HALVES * len(FLOWS))]
    strips = scratch[36 + 7 * HALVES * len(FLOWS) :]
    y, z, x, pair, core = place()
    rows, feat = inputs.shape
    cut = feat // HALVES
    right, left, opposite, other = turn(x, 1), turn(x, 3), turn(x, 2), 1 - pair
    to_pair = device(y, z, x, other, core)
    to_core = device(y, z, x, pair, 1 - core)
    peer_y = {by: device(turn(y, by), z, x, pair, core) for by in (1, 2, 3)}
    peer_z = {by: device(y, turn(z, by), x, pair, core) for by in (1, 2, 3)}
    peer_x = {by: device(y, z, turn(x, by), pair, core) for by in (1, 2, 3)}
    to_right, to_left = peer_x[1], peer_x[3]
    met = [to_pair, to_core] + [
        peer[by] for peer in (peer_y, peer_z, peer_x) for by in (1, 2, 3)
    ]
    barrier = pltpu.get_barrier_semaphore()
    for peer in met:
        pl.semaphore_signal(barrier, inc=1, device_id=peer, device_id_type=pl.DeviceIdType.MESH)
    post = Post(send_sem, recv_sem)
    peers = {"y": peer_y, "z": peer_z}
    own = {"y": y, "z": z}

    loads = []

    def load(src, dst):
        copy = pltpu.make_async_copy(src, dst, load_sem.at[len(loads)])
        copy.start()
        loads.append(copy)
        return copy

    half = rows // 2
    first = [load(w_neigh_in, w_neigh), load(inv_in, inv)]
    parts = []
    for h in range(2):
        span = pl.ds(h * half, half)
        parts.append(
            [load(preact_in.at[span], preact.at[span]), load(grad_out_in.at[span], grad_out.at[span])]
        )
    later = [load(w_self_in, w_self), load(inputs_in, inputs), load(aggregated_in, aggregated)]
    slots = blocks_in.shape[0]
    given = [
        load(rows_in, block_rows),
        load(cols_in, block_cols),
        load(count_in, block_count),
    ]
    fetched = load(blocks_in, blocks.at[pl.ds(0, slots)])

    per_shard = rows // EDGE

    def part(at_x, at_pair, at_core, h):
        shard = (at_x * 2 + at_pair) * 2 + at_core
        return pl.ds(shard * per_shard + h * (per_shard // 2), per_shard // 2)

    def gather(f):
        def send(where, peer):
            return post.send(strips[f].at[where], strips[f].at[where], peer)

        passed = []

        def arrived(copy, at_x, at_pair, h):
            copy.wait_recv()
            where = part(at_x, at_pair, core, h)
            passed.append(send(where, to_core))
            return where

        own_right, own_left, own_pair = {}, {}, {}
        for h in range(2):
            mine = part(x, pair, core, h)
            own_right[h] = send(mine, to_right)
            own_left[h] = send(mine, to_left)
            own_pair[h] = send(mine, to_pair)
            passed.append(send(mine, to_core))
            yield
        far_0 = send(arrived(own_right[0], left, pair, 0), to_right)
        arrived(own_left[0], right, pair, 0)
        yield
        where = arrived(own_pair[0], x, other, 0)
        other_right_0, other_left_0 = send(where, to_right), send(where, to_left)
        yield
        far_1 = send(arrived(own_left[1], right, pair, 1), to_left)
        arrived(own_right[1], left, pair, 1)
        yield
        where = arrived(own_pair[1], x, other, 1)
        other_right_1, other_left_1 = send(where, to_right), send(where, to_left)
        yield
        far_pair_0 = send(arrived(far_0, opposite, pair, 0), to_pair)
        far_pair_1 = send(arrived(far_1, opposite, pair, 1), to_pair)
        yield
        arrived(other_right_0, left, other, 0)
        arrived(other_left_0, right, other, 0)
        yield
        arrived(other_right_1, left, other, 1)
        arrived(other_left_1, right, other, 1)
        yield
        arrived(far_pair_0, opposite, other, 0)
        arrived(far_pair_1, opposite, other, 1)
        for copy in passed:
            copy.wait_recv()

    def product(f):
        for begin in range(0, PAIRS, PART):

            def body(u, total):
                for i in range(STRIDE):
                    at = begin + u * STRIDE + i
                    pick = (lists[0, 2 * at], lists[0, 2 * at + 1])
                    line = (lists[1, 2 * at], lists[1, 2 * at + 1])
                    go_on = lists[2, at] == 1
                    total = jnp.where(go_on, total, jnp.zeros_like(total)) + lax.dot_general(
                        jnp.concatenate([blocks[pick[0]], blocks[pick[1]]], axis=0),
                        jnp.concatenate([strips[f][line[0]], strips[f][line[1]]], axis=0),
                        (((0,), (0,)), ((), ())),
                        preferred_element_type=F32,
                    )
                    prefix[at] = total
                return total

            before = prefix[begin - 1] if begin else jnp.zeros((EDGE, cut), F32)
            lax.fori_loop(0, PART // STRIDE, body, before)
            yield

        def leave(g, carry):
            for i in range(4):
                at = g * 4 + i
                span = pl.ds(pl.multiple_of(at * EDGE, EDGE), EDGE)
                partial[f, span, :] = prefix[lists[3, at]].astype(BF16)
            return carry

        lax.fori_loop(0, TILES // 4, leave, 0)

    def flow(refs, f, first, second, offset, span):
        via_a, left_a, right_a, sum_a, hold, via_b, side_b = refs
        h = span // 2
        halves = (slice(0, h), slice(h, span))
        ahead_a, back_a = peers[first][1], peers[first][3]
        ahead_b, back_b = peers[second][1], peers[second][3]
        order = (2, 1, 3, 0)

        def piece(by_a, by_b, k):
            at = {first: turn(own[first], by_a), second: turn(own[second], by_b)}
            start = (at["y"] * 4 + at["z"]) * rows + offset
            if k is None:
                return pl.ds(pl.multiple_of(start, 128), span)
            return pl.ds(pl.multiple_of(start + k * h, 64), h)

        far, near = {}, {}

        def launch(i):
            b = order[i]
            far[i] = (
                post.send(partial.at[f, piece(2, b, 0)], via_a.at[i, 0], ahead_a),
                post.send(partial.at[f, piece(2, b, 1)], via_a.at[i, 1], back_a),
            )
            near[i] = [
                post.send(partial.at[f, piece(1, b, 1)], left_a.at[i, pl.ds(h, h)], ahead_a),
                post.send(partial.at[f, piece(3, b, 0)], right_a.at[i, pl.ds(0, h)], back_a),
            ]

        def relay(i):
            b = order[i]
            far[i][0].wait_recv()
            sum_a[i, 0] = (
                via_a[i, 0].astype(F32) + partial[f, piece(1, b, 0), :].astype(F32)
            ).astype(BF16)
            near[i].append(post.send(sum_a.at[i, 0], left_a.at[i, pl.ds(0, h)], ahead_a))
            far[i][1].wait_recv()
            sum_a[i, 1] = (
                via_a[i, 1].astype(F32) + partial[f, piece(3, b, 1), :].astype(F32)
            ).astype(BF16)
            near[i].append(post.send(sum_a.at[i, 1], right_a.at[i, pl.ds(h, h)], back_a))

        def close(i):
            for copy in near[i]:
                copy.wait_recv()
            return (
                partial[f, piece(0, order[i], None), :].astype(F32)
                + left_a[i].astype(F32)
                + right_a[i].astype(F32)
            )

        launch(0)
        launch(1)
        yield
        sent_b = []
        for i in range(5):
            if i < 4:
                relay(i)
                if i + 2 < 4:
                    launch(i + 2)
                yield
            if i == 0:
                continue
            done = close(i - 1)
            if i == 1:
                hold[0] = done.astype(BF16)
                far_b = (
                    post.send(hold.at[0, pl.ds(0, h)], via_b.at[0], ahead_b),
                    post.send(hold.at[0, pl.ds(h, h)], via_b.at[1], back_b),
                )
            elif i == 2:
                hold[1, pl.ds(h, h), :] = done[halves[1], :].astype(BF16)
                sent_b.append(
                    post.send(hold.at[1, pl.ds(h, h)], side_b.at[0, pl.ds(h, h)], ahead_b)
                )
                far_b[0].wait_recv()
                hold[1, pl.ds(0, h), :] = (done[halves[0], :] + via_b[0].astype(F32)).astype(BF16)
                sent_b.append(
                    post.send(hold.at[1, pl.ds(0, h)], side_b.at[0, pl.ds(0, h)], ahead_b)
                )
            elif i == 3:
                hold[2, pl.ds(0, h), :] = done[halves[0], :].astype(BF16)
                sent_b.append(
                    post.send(hold.at[2, pl.ds(0, h)], side_b.at[1, pl.ds(0, h)], back_b)
                )
                far_b[1].wait_recv()
                hold[2, pl.ds(h, h), :] = (done[halves[1], :] + via_b[1].astype(F32)).astype(BF16)
                sent_b.append(
                    post.send(hold.at[2, pl.ds(h, h)], side_b.at[1, pl.ds(h, h)], back_b)
                )
            else:
                done = done + self_term[pl.ds(offset, span), f * cut : (f + 1) * cut]
                yield
                for copy in sent_b:
                    copy.wait_recv()
                out[pl.ds(offset, span), f * cut : (f + 1) * cut] = (
                    done + side_b[0].astype(F32) + side_b[1].astype(F32)
                ).astype(BF16)
            yield

    def weight_sums():
        copies = [
            post.send(shares_y.at[turn(y, by)], from_y.at[y], peer_y[by]) for by in (1, 2, 3)
        ]
        from_y[y] = shares_y[y]
        yield
        for copy in copies:
            copy.wait_recv()
        total_y = sum(from_y[i].astype(F32) for i in range(4))
        for q in range(4):
            shares_z[q, :small, :] = total_y[q * small : (q + 1) * small, :].astype(BF16)
            shares_z[q, small:, :] = total_y[tall:, :].astype(BF16)
        copies = [
            post.send(shares_z.at[turn(z, by)], from_z.at[z], peer_z[by]) for by in (1, 2, 3)
        ]
        from_z[z] = shares_z[z]
        yield
        for copy in copies:
            copy.wait_recv()
        total_z = sum(from_z[i].astype(F32) for i in range(4))
        for q in range(4):
            shares_x[q, :PAD, :] = total_z[q * PAD : (q + 1) * PAD, :]
            shares_x[q, PAD:, :] = total_z[4 * PAD : 5 * PAD, :]
        copies = [
            post.send(shares_x.at[turn(x, by)], from_x.at[x], peer_x[by]) for by in (1, 2, 3)
        ]
        from_x[x] = shares_x[x]
        yield
        for copy in copies:
            copy.wait_recv()
        work_a[...] = from_x[0] + from_x[1] + from_x[2] + from_x[3]
        copy = post.send(work_a, from_core, to_core)
        yield
        copy.wait_recv()
        work_b[...] = work_a[...] + from_core[...]
        copy = post.send(work_b, from_pair, to_pair)
        yield
        copy.wait_recv()
        done = work_b[...] + from_pair[...]
        bias[...] = done[PAD:, :]
        by_z[z] = done[:PAD, :]
        copies = [post.send(by_z.at[z], by_z.at[z], peer_z[by]) for by in (1, 2, 3)]
        yield
        for copy in copies:
            copy.wait_recv()
        by_y[y] = by_z[...]
        copies = [post.send(by_z, by_y.at[y], peer_y[by]) for by in (1, 2, 3)]
        yield
        for copy in copies:
            copy.wait_recv()
        by_x[x] = by_y[...]
        copies = [post.send(by_y, by_x.at[x], peer_x[by]) for by in (1, 2, 3)]
        yield
        for copy in copies:
            copy.wait_recv()
        for at_y in range(4):
            for at_z in range(4):
                for at_x in range(4):
                    first = ((at_y * 4 + at_z) * 4 + at_x) * PAD
                    weights[first : first + PAD, :] = by_x[at_x, at_y, at_z]

    def step(one, count=1):
        for unused in range(count):
            if next(one, "end") == "end":
                return False
        return True

    gathers = [gather(f) for f in range(HALVES)]
    for copy in first:
        copy.wait()
    scales = inv[...].astype(F32).reshape(rows // EDGE, EDGE)
    for h in range(2):
        for copy in parts[h]:
            copy.wait()
        base = h * half
        grads = grad_out[base : base + half, :]
        masked = jnp.where(preact[base : base + half, :] > 0, grads, jnp.zeros_like(grads))
        masked_ref[base : base + half, :] = masked
        projected = lax.dot_general(
            masked, w_neigh[...], (((1,), (1,)), ((), ())), preferred_element_type=F32
        )
        for t in range(half // EDGE):
            at = h * (half // EDGE) + t
            scaled = (projected[t * EDGE : (t + 1) * EDGE, :] * stand(scales[at : at + 1, :])).astype(BF16)
            mine = ((x * 2 + pair) * 2 + core) * per_shard + at
            for f in range(HALVES):
                strips[f][mine] = scaled[:, f * cut : (f + 1) * cut]
        if h == 0:
            pl.semaphore_wait(barrier, len(met))
        step(gathers[0])
    for f in range(1, HALVES):
        step(gathers[f], 2)

    tall = 2 * feat // 4
    small = tall // 4

    def sort_chore():
        blocks[slots] = jnp.zeros((EDGE, EDGE), BF16)
        prefix[PAIRS] = jnp.zeros((EDGE, cut), F32)
        for copy in given:
            copy.wait()
        spots = slots + -slots % EDGE
        spot = iota((1, spots), 1)

        def line_up(u, rows_of):
            col_row, row_row = rows_of
            for i in range(8):
                at = u * 8 + i
                col_row = jnp.where(spot == at, block_cols[at], col_row)
                row_row = jnp.where(spot == at, block_rows[at], row_row)
            return col_row, row_row

        blank = jnp.zeros((1, spots), I32)
        col_row, row_row = lax.fori_loop(0, slots // 8, line_up, (blank, blank))
        live = spot < block_count[0, 0]
        order_slots(jnp.where(live, col_row, EDGE - 1), row_row, lists_v, slots)
        return load(lists_v, lists)

    def weight_chore(which, factor):
        result = lax.dot_general(
            factor[...], masked_ref[...], (((0,), (0,)), ((), ())), preferred_element_type=F32
        )
        for q in range(2):
            shares_y[which * 2 + q, :tall, :] = result[q * tall : (q + 1) * tall, :].astype(BF16)

    def bias_chore():
        bias_part = jnp.sum(masked_ref[...].astype(F32), axis=0, keepdims=True)
        for q in range(4):
            shares_y[q, tall:, :] = jnp.broadcast_to(bias_part, (2 * PAD, feat)).astype(BF16)

    sums = weight_sums()
    listed = sort_chore()
    step(gathers[0], 2)
    later[0].wait()
    self_term[...] = lax.dot_general(
        masked_ref[...], w_self[...], (((1,), (1,)), ((), ())), preferred_element_type=F32
    )
    step(gathers[0], 2)
    later[1].wait()
    weight_chore(0, inputs)
    step(gathers[0])
    step(gathers[1])
    later[2].wait()
    weight_chore(1, aggregated)
    step(gathers[1])
    bias_chore()
    step(sums)
    step(gathers[0])
    step(gathers[1])
    step(gathers[0])
    step(gathers[1])
    step(gathers[0])
    listed.wait()
    fetched.wait()

    flows = []
    turns = 0
    for f in range(HALVES):
        work = product(f)
        busy = True
        while busy:
            busy = step(work)
            if f + 1 < HALVES:
                step(gathers[f + 1])
            flows = [one for one in flows if step(one)]
            turns += 1
            if turns in SUM_TURNS:
                step(sums)
        if f + 1 < HALVES:
            while step(gathers[f + 1]):
                pass
        flows += [
            flow(flow_refs[f * len(FLOWS) + i], f, *spec) for i, spec in enumerate(FLOWS)
        ]
        flows = [one for one in flows if step(one)]
    while flows:
        flows = [one for one in flows if step(one)]
        turns += 1
        if turns in SUM_TURNS:
            step(sums)
    while step(sums):
        pass
    results = [
        load(out, out_hbm), load(weights, weights_hbm), load(bias, bias_hbm)
    ]
    post.finish()
    for copy in results:
        copy.wait()


def leave_kernel(
    grads, weights, bias, grads_out, self_out, neigh_out, bias_out,
    grads_v, self_v, neigh_v, bias_v, sem_in, sem_out,
):
    feat = weights.shape[1]
    moves = (
        (weights.at[pl.ds(0, feat)], self_v, self_v, self_out),
        (weights.at[pl.ds(feat, feat)], neigh_v, neigh_v, neigh_out),
        (grads, grads_v, grads_v, grads_out),
        (bias, bias_v, bias_v.at[pl.ds(0, 1)], bias_out),
    )
    come = [pltpu.make_async_copy(m[0], m[1], sem_in.at[i]) for i, m in enumerate(moves)]
    go = [pltpu.make_async_copy(m[2], m[3], sem_out.at[i]) for i, m in enumerate(moves)]
    for copy in come:
        copy.start()
    for arrival, departure in zip(come, go):
        arrival.wait()
        departure.start()
    for copy in go:
        copy.wait()


def local(
    inputs, aggregated, grad_out, preact, inv_degree, w_self, w_neigh,
    blocks, block_rows, block_cols, block_count,
):
    rows, feat = inputs.shape
    cut = feat // HALVES
    strip_rows = rows * lax.axis_size("col")
    group_rows = rows * lax.axis_size("row")
    hbm = pl.BlockSpec(memory_space=pltpu.HBM)
    dma = pltpu.SemaphoreType.DMA
    slots = blocks.shape[0]
    tall = 2 * feat // 4
    small = tall // 4
    whole = pltpu.VMEM((rows, feat), BF16)
    square = pltpu.VMEM((feat, feat), BF16)
    two = (2 * PAD, feat)
    sends = HALVES * (30 + 30 * len(FLOWS)) + 20
    scratch = [
        whole, whole, whole, whole, square, square, whole, pltpu.VMEM((rows, feat), F32),
        pltpu.VMEM((slots + 1, EDGE, EDGE), BF16),
        pltpu.VMEM((PAIRS + 1, EDGE, cut), F32),
        pltpu.VMEM((HALVES, group_rows, cut), BF16),
        pltpu.VMEM((8, 512), I32),
        pltpu.SMEM((8, 512), I32),
        pltpu.VMEM((4, tall + 2 * PAD, feat), BF16),
        pltpu.VMEM((4, tall + 2 * PAD, feat), BF16),
        pltpu.VMEM((4, small + 2 * PAD, feat), BF16),
        pltpu.VMEM((4, small + 2 * PAD, feat), BF16),
        pltpu.VMEM((4,) + two, F32),
        pltpu.VMEM((4,) + two, F32),
        pltpu.VMEM(two, F32),
        pltpu.VMEM(two, F32),
        pltpu.VMEM(two, F32),
        pltpu.VMEM(two, F32),
        pltpu.VMEM((4, PAD, feat), F32),
        pltpu.VMEM((4, 4, PAD, feat), F32),
        pltpu.VMEM((4, 4, 4, PAD, feat), F32),
        pltpu.VMEM((rows,), BF16),
        pltpu.SMEM((slots,), I32),
        pltpu.SMEM((slots,), I32),
        pltpu.SMEM((1, 1), I32),
        whole,
        pltpu.VMEM((2 * feat, feat), F32),
        pltpu.VMEM((PAD, feat), F32),
        dma((sends,)),
        dma((sends,)),
        dma((20,)),
    ]
    for unused in range(HALVES):
        for unused_a, unused_b, unused_c, span in FLOWS:
            scratch += [
                pltpu.VMEM((4, 2, span // 2, cut), BF16),
                pltpu.VMEM((4, span, cut), BF16),
                pltpu.VMEM((4, span, cut), BF16),
                pltpu.VMEM((4, 2, span // 2, cut), BF16),
                pltpu.VMEM((3, span, cut), BF16),
                pltpu.VMEM((2, span // 2, cut), BF16),
                pltpu.VMEM((2, span, cut), BF16),
            ]
    scratch += [pltpu.VMEM((strip_rows // EDGE, EDGE, cut), BF16)] * HALVES
    results = pl.pallas_call(
        layer_kernel,
        out_shape=(
            jax.ShapeDtypeStruct((rows, feat), BF16),
            jax.ShapeDtypeStruct((2 * feat, feat), F32),
            jax.ShapeDtypeStruct((PAD, feat), F32),
        ),
        in_specs=[hbm] * 11,
        out_specs=(hbm, hbm, hbm),
        scratch_shapes=scratch,
        compiler_params=pltpu.CompilerParams(
            collective_id=0, has_side_effects=True, vmem_limit_bytes=LIMIT * 2**20
        ),
        name="layer",
    )(
        inputs, aggregated, grad_out, preact, inv_degree, w_self, w_neigh,
        blocks, block_rows, block_cols, block_count,
    )
    square_out = pltpu.VMEM((feat, feat), F32)
    grad_inputs, grad_self, grad_neigh, grad_bias = pl.pallas_call(
        leave_kernel,
        out_shape=(
            jax.ShapeDtypeStruct((rows, feat), BF16),
            jax.ShapeDtypeStruct((feat, feat), F32),
            jax.ShapeDtypeStruct((feat, feat), F32),
            jax.ShapeDtypeStruct((1, feat), F32),
        ),
        in_specs=[hbm] * 3,
        out_specs=[hbm] * 4,
        scratch_shapes=[
            whole, square_out, square_out, pltpu.VMEM((PAD, feat), F32), dma((4,)), dma((4,)),
        ],
        compiler_params=pltpu.CompilerParams(vmem_limit_bytes=LIMIT * 2**20),
        name="leave",
    )(*results)
    return grad_inputs, grad_self, grad_neigh, grad_bias.reshape(feat)


def solution(mesh):
    both = ("row", "col")
    return jax.shard_map(
        local,
        mesh=mesh,
        in_specs=(
            P(both, None), P(both, None), P(both, None), P(both, None), P(both),
            P(), P(),
            P(both, None, None), P(both), P(both), P("row", "col"),
        ),
        out_specs=(P(both, None), P(), P(), P()),
        check_vma=False,
    )
```

```python
import functools

import jax
import jax.numpy as jnp
from jax import lax
from jax.experimental import pallas as pl
from jax.experimental.pallas import tpu as pltpu
from jax.sharding import PartitionSpec as P

EDGE = 128
HALVES = 2
TILES = 64
I32 = jnp.int32
F32 = jnp.float32
BF16 = jnp.bfloat16
FLOWS = (("y", "z", 0, 384), ("z", "y", 384, 128))
PAD = 8
LIMIT = 62
SUM_TURNS = (3, 6, 8, 10, 12, 15, 18, 21)
PAIRS = 200
STRIDE = 20
PART = 40


def place():
    r = lax.axis_index("row")
    c = lax.axis_index("col")
    return r // 4, r % 4, c // 4, (c // 2) % 2, c % 2


def device(y, z, x, pair, core):
    return {"row": y * 4 + z, "col": x * 4 + pair * 2 + core}


def turn(v, by):
    return (v + by) % 4


class Post:
    def __init__(self, send_sem, recv_sem):
        self.send_sem = send_sem
        self.recv_sem = recv_sem
        self.sent = []

    def send(self, src, dst, peer):
        at = len(self.sent)
        copy = pltpu.make_async_remote_copy(
            src_ref=src,
            dst_ref=dst,
            send_sem=self.send_sem.at[at],
            recv_sem=self.recv_sem.at[at],
            device_id=peer,
            device_id_type=pl.DeviceIdType.MESH,
        )
        copy.start()
        self.sent.append(copy)
        return copy

    def finish(self):
        for copy in self.sent:
            copy.wait_send()


def count_of(condition):
    return jnp.where(condition, 1, 0).astype(I32)


def iota(shape, axis):
    return lax.broadcasted_iota(I32, shape, axis)


def stand(row):
    eye = iota((EDGE, EDGE), 0) == iota((EDGE, EDGE), 1)
    parts = []
    for t in range(row.shape[1] // EDGE):
        wide = jnp.broadcast_to(row[:, t * EDGE : (t + 1) * EDGE], (EDGE, EDGE))
        parts.append(jnp.sum(jnp.where(eye, wide, jnp.zeros_like(wide)), axis=1, keepdims=True))
    return jnp.concatenate(parts, axis=0)


def order_slots(col_row, row_row, lists, empty):
    slots, spots = col_row.shape[1], lists.shape[1]
    col, row = stand(col_row), stand(row_row)
    earlier = iota((slots, slots), 1) < iota((slots, slots), 0)
    equal = jnp.broadcast_to(col_row, (slots, slots)) == jnp.broadcast_to(col, (slots, slots))
    within = jnp.sum(count_of(equal & earlier), axis=1, keepdims=True)
    hit = jnp.broadcast_to(col, (slots, EDGE)) == iota((slots, EDGE), 1)
    pairs_row = (jnp.sum(count_of(hit), axis=0, keepdims=True) + 1) // 2
    pairs_row = jnp.where(iota((1, EDGE), 1) < TILES, pairs_row, 0)
    pairs_col = stand(pairs_row)
    square = (EDGE, EDGE)
    start_col = jnp.sum(
        jnp.where(iota(square, 1) < iota(square, 0), jnp.broadcast_to(pairs_row, square), 0),
        axis=1, keepdims=True,
    )
    start_row = jnp.sum(
        jnp.where(iota(square, 0) < iota(square, 1), jnp.broadcast_to(pairs_col, square), 0),
        axis=0, keepdims=True,
    )
    start = jnp.sum(
        jnp.where(hit, jnp.broadcast_to(start_row, (slots, EDGE)), 0), axis=1, keepdims=True
    )
    spot = jnp.where(col < TILES, 2 * start + within, -1)
    here = jnp.broadcast_to(spot, (slots, spots)) == iota((slots, spots), 1)
    lists[0:1, :] = empty + jnp.sum(
        jnp.where(here, iota((slots, spots), 0) - empty, 0), axis=0, keepdims=True
    )
    lists[1:2, :] = jnp.sum(
        jnp.where(here, jnp.broadcast_to(row, (slots, spots)), 0), axis=0, keepdims=True
    )
    begins = (jnp.broadcast_to(start_col, (EDGE, spots)) == iota((EDGE, spots), 1)) & (
        jnp.broadcast_to(pairs_col, (EDGE, spots)) > 0
    )
    lists[2:3, :] = 1 - jnp.sum(count_of(begins), axis=0, keepdims=True)
    last = jnp.where(pairs_row > 0, start_row + pairs_row - 1, PAIRS)
    lists[3:4, :] = jnp.concatenate([last, jnp.zeros((1, spots - EDGE), I32)], axis=1)
    lists[4:8, :] = jnp.zeros((4, spots), I32)


def layer_kernel(
    inputs_in, aggregated_in, grad_out_in, preact_in, inv_in, w_self_in, w_neigh_in,
    blocks_in, rows_in, cols_in, count_in, out_hbm, weights_hbm, bias_hbm, *scratch,
):
    (
        inputs, aggregated, grad_out, preact, w_self, w_neigh, masked_ref, self_term,
        blocks, prefix, partial, lists_v, lists,
        shares_y, from_y, shares_z, from_z, shares_x, from_x,
        work_a, from_core, work_b, from_pair, by_z, by_y, by_x,
        inv, block_rows, block_cols, block_count, out, weights, bias,
        send_sem, recv_sem, load_sem,
    ) = scratch[:36]
    flow_refs = [scratch[36 + i * 7 : 43 + i * 7] for i in range(HALVES * len(FLOWS))]
    strips = scratch[36 + 7 * HALVES * len(FLOWS) :]
    y, z, x, pair, core = place()
    rows, feat = inputs.shape
    cut = feat // HALVES
    right, left, opposite, other = turn(x, 1), turn(x, 3), turn(x, 2), 1 - pair
    to_pair = device(y, z, x, other, core)
    to_core = device(y, z, x, pair, 1 - core)
    peer_y = {by: device(turn(y, by), z, x, pair, core) for by in (1, 2, 3)}
    peer_z = {by: device(y, turn(z, by), x, pair, core) for by in (1, 2, 3)}
    peer_x = {by: device(y, z, turn(x, by), pair, core) for by in (1, 2, 3)}
    to_right, to_left = peer_x[1], peer_x[3]
    met = [to_pair, to_core] + [
        peer[by] for peer in (peer_y, peer_z, peer_x) for by in (1, 2, 3)
    ]
    barrier = pltpu.get_barrier_semaphore()
    for peer in met:
        pl.semaphore_signal(barrier, inc=1, device_id=peer, device_id_type=pl.DeviceIdType.MESH)
    post = Post(send_sem, recv_sem)
    peers = {"y": peer_y, "z": peer_z}
    own = {"y": y, "z": z}

    loads = []

    def load(src, dst):
        copy = pltpu.make_async_copy(src, dst, load_sem.at[len(loads)])
        copy.start()
        loads.append(copy)
        return copy

    half = rows // 2
    first = [load(w_neigh_in, w_neigh), load(inv_in, inv)]
    parts = []
    for h in range(2):
        span = pl.ds(h * half, half)
        parts.append(
            [load(preact_in.at[span], preact.at[span]), load(grad_out_in.at[span], grad_out.at[span])]
        )
    later = [load(w_self_in, w_self), load(inputs_in, inputs), load(aggregated_in, aggregated)]
    slots = blocks_in.shape[0]
    given = [
        load(rows_in, block_rows),
        load(cols_in, block_cols),
        load(count_in, block_count),
    ]
    fetched = load(blocks_in, blocks.at[pl.ds(0, slots)])

    per_shard = rows // EDGE

    def part(at_x, at_pair, at_core, h):
        shard = (at_x * 2 + at_pair) * 2 + at_core
        return pl.ds(shard * per_shard + h * (per_shard // 2), per_shard // 2)

    def gather(f):
        def send(where, peer):
            return post.send(strips[f].at[where], strips[f].at[where], peer)

        passed = []

        def arrived(copy, at_x, at_pair, h):
            copy.wait_recv()
            where = part(at_x, at_pair, core, h)
            passed.append(send(where, to_core))
            return where

        own_right, own_left, own_pair = {}, {}, {}
        for h in range(2):
            mine = part(x, pair, core, h)
            own_right[h] = send(mine, to_right)
            own_left[h] = send(mine, to_left)
            own_pair[h] = send(mine, to_pair)
            passed.append(send(mine, to_core))
            yield
        far_0 = send(arrived(own_right[0], left, pair, 0), to_right)
        arrived(own_left[0], right, pair, 0)
        yield
        where = arrived(own_pair[0], x, other, 0)
        other_right_0, other_left_0 = send(where, to_right), send(where, to_left)
        yield
        far_1 = send(arrived(own_left[1], right, pair, 1), to_left)
        arrived(own_right[1], left, pair, 1)
        yield
        where = arrived(own_pair[1], x, other, 1)
        other_right_1, other_left_1 = send(where, to_right), send(where, to_left)
        yield
        far_pair_0 = send(arrived(far_0, opposite, pair, 0), to_pair)
        far_pair_1 = send(arrived(far_1, opposite, pair, 1), to_pair)
        yield
        arrived(other_right_0, left, other, 0)
        arrived(other_left_0, right, other, 0)
        yield
        arrived(other_right_1, left, other, 1)
        arrived(other_left_1, right, other, 1)
        yield
        arrived(far_pair_0, opposite, other, 0)
        arrived(far_pair_1, opposite, other, 1)
        for copy in passed:
            copy.wait_recv()

    def product(f):
        for begin in range(0, PAIRS, PART):

            def body(u, total):
                for i in range(STRIDE):
                    at = begin + u * STRIDE + i
                    pick = (lists[0, 2 * at], lists[0, 2 * at + 1])
                    line = (lists[1, 2 * at], lists[1, 2 * at + 1])
                    go_on = lists[2, at] == 1
                    total = jnp.where(go_on, total, jnp.zeros_like(total)) + lax.dot_general(
                        jnp.concatenate([blocks[pick[0]], blocks[pick[1]]], axis=0),
                        jnp.concatenate([strips[f][line[0]], strips[f][line[1]]], axis=0),
                        (((0,), (0,)), ((), ())),
                        preferred_element_type=F32,
                    )
                    prefix[at] = total
                return total

            before = prefix[begin - 1] if begin else jnp.zeros((EDGE, cut), F32)
            lax.fori_loop(0, PART // STRIDE, body, before)
            yield

        def leave(g, carry):
            for i in range(4):
                at = g * 4 + i
                span = pl.ds(pl.multiple_of(at * EDGE, EDGE), EDGE)
                partial[f, span, :] = prefix[lists[3, at]].astype(BF16)
            return carry

        lax.fori_loop(0, TILES // 4, leave, 0)

    def flow(refs, f, first, second, offset, span):
        via_a, left_a, right_a, sum_a, hold, via_b, side_b = refs
        h = span // 2
        halves = (slice(0, h), slice(h, span))
        ahead_a, back_a = peers[first][1], peers[first][3]
        ahead_b, back_b = peers[second][1], peers[second][3]
        order = (2, 1, 3, 0)

        def piece(by_a, by_b, k):
            at = {first: turn(own[first], by_a), second: turn(own[second], by_b)}
            start = (at["y"] * 4 + at["z"]) * rows + offset
            if k is None:
                return pl.ds(pl.multiple_of(start, 128), span)
            return pl.ds(pl.multiple_of(start + k * h, 64), h)

        far, near = {}, {}

        def launch(i):
            b = order[i]
            far[i] = (
                post.send(partial.at[f, piece(2, b, 0)], via_a.at[i, 0], ahead_a),
                post.send(partial.at[f, piece(2, b, 1)], via_a.at[i, 1], back_a),
            )
            near[i] = [
                post.send(partial.at[f, piece(1, b, 1)], left_a.at[i, pl.ds(h, h)], ahead_a),
                post.send(partial.at[f, piece(3, b, 0)], right_a.at[i, pl.ds(0, h)], back_a),
            ]

        def relay(i):
            b = order[i]
            far[i][0].wait_recv()
            sum_a[i, 0] = (
                via_a[i, 0].astype(F32) + partial[f, piece(1, b, 0), :].astype(F32)
            ).astype(BF16)
            near[i].append(post.send(sum_a.at[i, 0], left_a.at[i, pl.ds(0, h)], ahead_a))
            far[i][1].wait_recv()
            sum_a[i, 1] = (
                via_a[i, 1].astype(F32) + partial[f, piece(3, b, 1), :].astype(F32)
            ).astype(BF16)
            near[i].append(post.send(sum_a.at[i, 1], right_a.at[i, pl.ds(h, h)], back_a))

        def close(i):
            for copy in near[i]:
                copy.wait_recv()
            return (
                partial[f, piece(0, order[i], None), :].astype(F32)
                + left_a[i].astype(F32)
                + right_a[i].astype(F32)
            )

        launch(0)
        launch(1)
        yield
        sent_b = []
        for i in range(5):
            if i < 4:
                relay(i)
                if i + 2 < 4:
                    launch(i + 2)
                yield
            if i == 0:
                continue
            done = close(i - 1)
            if i == 1:
                hold[0] = done.astype(BF16)
                far_b = (
                    post.send(hold.at[0, pl.ds(0, h)], via_b.at[0], ahead_b),
                    post.send(hold.at[0, pl.ds(h, h)], via_b.at[1], back_b),
                )
            elif i == 2:
                hold[1, pl.ds(h, h), :] = done[halves[1], :].astype(BF16)
                sent_b.append(
                    post.send(hold.at[1, pl.ds(h, h)], side_b.at[0, pl.ds(h, h)], ahead_b)
                )
                far_b[0].wait_recv()
                hold[1, pl.ds(0, h), :] = (done[halves[0], :] + via_b[0].astype(F32)).astype(BF16)
                sent_b.append(
                    post.send(hold.at[1, pl.ds(0, h)], side_b.at[0, pl.ds(0, h)], ahead_b)
                )
            elif i == 3:
                hold[2, pl.ds(0, h), :] = done[halves[0], :].astype(BF16)
                sent_b.append(
                    post.send(hold.at[2, pl.ds(0, h)], side_b.at[1, pl.ds(0, h)], back_b)
                )
                far_b[1].wait_recv()
                hold[2, pl.ds(h, h), :] = (done[halves[1], :] + via_b[1].astype(F32)).astype(BF16)
                sent_b.append(
                    post.send(hold.at[2, pl.ds(h, h)], side_b.at[1, pl.ds(h, h)], back_b)
                )
            else:
                done = done + self_term[pl.ds(offset, span), f * cut : (f + 1) * cut]
                yield
                for copy in sent_b:
                    copy.wait_recv()
                out[pl.ds(offset, span), f * cut : (f + 1) * cut] = (
                    done + side_b[0].astype(F32) + side_b[1].astype(F32)
                ).astype(BF16)
            yield

    def weight_sums():
        copies = [
            post.send(shares_y.at[turn(y, by)], from_y.at[y], peer_y[by]) for by in (1, 2, 3)
        ]
        from_y[y] = shares_y[y]
        yield
        for copy in copies:
            copy.wait_recv()
        total_y = sum(from_y[i].astype(F32) for i in range(4))
        for q in range(4):
            shares_z[q, :small, :] = total_y[q * small : (q + 1) * small, :].astype(BF16)
            shares_z[q, small:, :] = total_y[tall:, :].astype(BF16)
        copies = [
            post.send(shares_z.at[turn(z, by)], from_z.at[z], peer_z[by]) for by in (1, 2, 3)
        ]
        from_z[z] = shares_z[z]
        yield
        for copy in copies:
            copy.wait_recv()
        total_z = sum(from_z[i].astype(F32) for i in range(4))
        for q in range(4):
            shares_x[q, :PAD, :] = total_z[q * PAD : (q + 1) * PAD, :]
            shares_x[q, PAD:, :] = total_z[4 * PAD : 5 * PAD, :]
        copies = [
            post.send(shares_x.at[turn(x, by)], from_x.at[x], peer_x[by]) for by in (1, 2, 3)
        ]
        from_x[x] = shares_x[x]
        yield
        for copy in copies:
            copy.wait_recv()
        work_a[...] = from_x[0] + from_x[1] + from_x[2] + from_x[3]
        copy = post.send(work_a, from_core, to_core)
        yield
        copy.wait_recv()
        work_b[...] = work_a[...] + from_core[...]
        copy = post.send(work_b, from_pair, to_pair)
        yield
        copy.wait_recv()
        done = work_b[...] + from_pair[...]
        bias[...] = done[PAD:, :]
        by_z[z] = done[:PAD, :]
        copies = [post.send(by_z.at[z], by_z.at[z], peer_z[by]) for by in (1, 2, 3)]
        yield
        for copy in copies:
            copy.wait_recv()
        by_y[y] = by_z[...]
        copies = [post.send(by_z, by_y.at[y], peer_y[by]) for by in (1, 2, 3)]
        yield
        for copy in copies:
            copy.wait_recv()
        by_x[x] = by_y[...]
        copies = [post.send(by_y, by_x.at[x], peer_x[by]) for by in (1, 2, 3)]
        yield
        for copy in copies:
            copy.wait_recv()
        for at_y in range(4):
            for at_z in range(4):
                for at_x in range(4):
                    first = ((at_y * 4 + at_z) * 4 + at_x) * PAD
                    weights[first : first + PAD, :] = by_x[at_x, at_y, at_z]

    def step(one, count=1):
        for unused in range(count):
            if next(one, "end") == "end":
                return False
        return True

    gathers = [gather(f) for f in range(HALVES)]
    for copy in first:
        copy.wait()
    scales = inv[...].astype(F32).reshape(rows // EDGE, EDGE)
    for h in range(2):
        for copy in parts[h]:
            copy.wait()
        base = h * half
        grads = grad_out[base : base + half, :]
        masked = jnp.where(preact[base : base + half, :] > 0, grads, jnp.zeros_like(grads))
        masked_ref[base : base + half, :] = masked
        projected = lax.dot_general(
            masked, w_neigh[...], (((1,), (1,)), ((), ())), preferred_element_type=F32
        )
        for t in range(half // EDGE):
            at = h * (half // EDGE) + t
            scaled = (projected[t * EDGE : (t + 1) * EDGE, :] * stand(scales[at : at + 1, :])).astype(BF16)
            mine = ((x * 2 + pair) * 2 + core) * per_shard + at
            for f in range(HALVES):
                strips[f][mine] = scaled[:, f * cut : (f + 1) * cut]
        if h == 0:
            pl.semaphore_wait(barrier, len(met))
        step(gathers[0])
    for f in range(1, HALVES):
        step(gathers[f], 2)

    tall = 2 * feat // 4
    small = tall // 4

    def sort_chore():
        blocks[slots] = jnp.zeros((EDGE, EDGE), BF16)
        prefix[PAIRS] = jnp.zeros((EDGE, cut), F32)
        for copy in given:
            copy.wait()
        spots = slots + -slots % EDGE
        spot = iota((1, spots), 1)

        def line_up(u, rows_of):
            col_row, row_row = rows_of
            for i in range(8):
                at = u * 8 + i
                col_row = jnp.where(spot == at, block_cols[at], col_row)
                row_row = jnp.where(spot == at, block_rows[at], row_row)
            return col_row, row_row

        blank = jnp.zeros((1, spots), I32)
        col_row, row_row = lax.fori_loop(0, slots // 8, line_up, (blank, blank))
        live = spot < block_count[0, 0]
        order_slots(jnp.where(live, col_row, EDGE - 1), row_row, lists_v, slots)
        return load(lists_v, lists)

    def weight_chore(which, factor):
        result = lax.dot_general(
            factor[...], masked_ref[...], (((0,), (0,)), ((), ())), preferred_element_type=F32
        )
        for q in range(2):
            shares_y[which * 2 + q, :tall, :] = result[q * tall : (q + 1) * tall, :].astype(BF16)

    def bias_chore():
        bias_part = jnp.sum(masked_ref[...].astype(F32), axis=0, keepdims=True)
        for q in range(4):
            shares_y[q, tall:, :] = jnp.broadcast_to(bias_part, (2 * PAD, feat)).astype(BF16)

    sums = weight_sums()
    listed = sort_chore()
    step(gathers[0], 2)
    later[0].wait()
    self_term[...] = lax.dot_general(
        masked_ref[...], w_self[...], (((1,), (1,)), ((), ())), preferred_element_type=F32
    )
    step(gathers[0], 2)
    later[1].wait()
    weight_chore(0, inputs)
    step(gathers[0])
    step(gathers[1])
    later[2].wait()
    weight_chore(1, aggregated)
    step(gathers[1])
    bias_chore()
    step(sums)
    step(gathers[0])
    step(gathers[1])
    step(gathers[0])
    step(gathers[1])
    step(gathers[0])
    listed.wait()
    fetched.wait()

    flows = []
    turns = 0
    for f in range(HALVES):
        work = product(f)
        busy = True
        while busy:
            busy = step(work)
            if f + 1 < HALVES:
                step(gathers[f + 1])
            if turns % 2:
                flows = [one for one in flows if step(one)]
            turns += 1
            if turns in SUM_TURNS:
                step(sums)
        if f + 1 < HALVES:
            while step(gathers[f + 1]):
                pass
        flows += [
            flow(flow_refs[f * len(FLOWS) + i], f, *spec) for i, spec in enumerate(FLOWS)
        ]
        flows = [one for one in flows if step(one)]
    while flows:
        flows = [one for one in flows if step(one)]
        turns += 1
        if turns in SUM_TURNS:
            step(sums)
    while step(sums):
        pass
    results = [
        load(out, out_hbm), load(weights, weights_hbm), load(bias, bias_hbm)
    ]
    post.finish()
    for copy in results:
        copy.wait()


def leave_kernel(
    grads, weights, bias, grads_out, self_out, neigh_out, bias_out,
    grads_v, self_v, neigh_v, bias_v, sem_in, sem_out,
):
    feat = weights.shape[1]
    moves = (
        (weights.at[pl.ds(0, feat)], self_v, self_v, self_out),
        (weights.at[pl.ds(feat, feat)], neigh_v, neigh_v, neigh_out),
        (grads, grads_v, grads_v, grads_out),
        (bias, bias_v, bias_v.at[pl.ds(0, 1)], bias_out),
    )
    come = [pltpu.make_async_copy(m[0], m[1], sem_in.at[i]) for i, m in enumerate(moves)]
    go = [pltpu.make_async_copy(m[2], m[3], sem_out.at[i]) for i, m in enumerate(moves)]
    for copy in come:
        copy.start()
    for arrival, departure in zip(come, go):
        arrival.wait()
        departure.start()
    for copy in go:
        copy.wait()


def local(
    inputs, aggregated, grad_out, preact, inv_degree, w_self, w_neigh,
    blocks, block_rows, block_cols, block_count,
):
    rows, feat = inputs.shape
    cut = feat // HALVES
    strip_rows = rows * lax.axis_size("col")
    group_rows = rows * lax.axis_size("row")
    hbm = pl.BlockSpec(memory_space=pltpu.HBM)
    dma = pltpu.SemaphoreType.DMA
    slots = blocks.shape[0]
    tall = 2 * feat // 4
    small = tall // 4
    whole = pltpu.VMEM((rows, feat), BF16)
    square = pltpu.VMEM((feat, feat), BF16)
    two = (2 * PAD, feat)
    sends = HALVES * (30 + 30 * len(FLOWS)) + 20
    scratch = [
        whole, whole, whole, whole, square, square, whole, pltpu.VMEM((rows, feat), F32),
        pltpu.VMEM((slots + 1, EDGE, EDGE), BF16),
        pltpu.VMEM((PAIRS + 1, EDGE, cut), F32),
        pltpu.VMEM((HALVES, group_rows, cut), BF16),
        pltpu.VMEM((8, 512), I32),
        pltpu.SMEM((8, 512), I32),
        pltpu.VMEM((4, tall + 2 * PAD, feat), BF16),
        pltpu.VMEM((4, tall + 2 * PAD, feat), BF16),
        pltpu.VMEM((4, small + 2 * PAD, feat), BF16),
        pltpu.VMEM((4, small + 2 * PAD, feat), BF16),
        pltpu.VMEM((4,) + two, F32),
        pltpu.VMEM((4,) + two, F32),
        pltpu.VMEM(two, F32),
        pltpu.VMEM(two, F32),
        pltpu.VMEM(two, F32),
        pltpu.VMEM(two, F32),
        pltpu.VMEM((4, PAD, feat), F32),
        pltpu.VMEM((4, 4, PAD, feat), F32),
        pltpu.VMEM((4, 4, 4, PAD, feat), F32),
        pltpu.VMEM((rows,), BF16),
        pltpu.SMEM((slots,), I32),
        pltpu.SMEM((slots,), I32),
        pltpu.SMEM((1, 1), I32),
        whole,
        pltpu.VMEM((2 * feat, feat), F32),
        pltpu.VMEM((PAD, feat), F32),
        dma((sends,)),
        dma((sends,)),
        dma((20,)),
    ]
    for unused in range(HALVES):
        for unused_a, unused_b, unused_c, span in FLOWS:
            scratch += [
                pltpu.VMEM((4, 2, span // 2, cut), BF16),
                pltpu.VMEM((4, span, cut), BF16),
                pltpu.VMEM((4, span, cut), BF16),
                pltpu.VMEM((4, 2, span // 2, cut), BF16),
                pltpu.VMEM((3, span, cut), BF16),
                pltpu.VMEM((2, span // 2, cut), BF16),
                pltpu.VMEM((2, span, cut), BF16),
            ]
    scratch += [pltpu.VMEM((strip_rows // EDGE, EDGE, cut), BF16)] * HALVES
    results = pl.pallas_call(
        layer_kernel,
        out_shape=(
            jax.ShapeDtypeStruct((rows, feat), BF16),
            jax.ShapeDtypeStruct((2 * feat, feat), F32),
            jax.ShapeDtypeStruct((PAD, feat), F32),
        ),
        in_specs=[hbm] * 11,
        out_specs=(hbm, hbm, hbm),
        scratch_shapes=scratch,
        compiler_params=pltpu.CompilerParams(
            collective_id=0, has_side_effects=True, vmem_limit_bytes=LIMIT * 2**20
        ),
        name="layer",
    )(
        inputs, aggregated, grad_out, preact, inv_degree, w_self, w_neigh,
        blocks, block_rows, block_cols, block_count,
    )
    square_out = pltpu.VMEM((feat, feat), F32)
    grad_inputs, grad_self, grad_neigh, grad_bias = pl.pallas_call(
        leave_kernel,
        out_shape=(
            jax.ShapeDtypeStruct((rows, feat), BF16),
            jax.ShapeDtypeStruct((feat, feat), F32),
            jax.ShapeDtypeStruct((feat, feat), F32),
            jax.ShapeDtypeStruct((1, feat), F32),
        ),
        in_specs=[hbm] * 3,
        out_specs=[hbm] * 4,
        scratch_shapes=[
            whole, square_out, square_out, pltpu.VMEM((PAD, feat), F32), dma((4,)), dma((4,)),
        ],
        compiler_params=pltpu.CompilerParams(vmem_limit_bytes=LIMIT * 2**20),
        name="leave",
    )(*results)
    return grad_inputs, grad_self, grad_neigh, grad_bias.reshape(feat)


def solution(mesh):
    both = ("row", "col")
    return jax.shard_map(
        local,
        mesh=mesh,
        in_specs=(
            P(both, None), P(both, None), P(both, None), P(both, None), P(both),
            P(), P(),
            P(both, None, None), P(both), P(both), P("row", "col"),
        ),
        out_specs=(P(both, None), P(), P(), P()),
        check_vma=False,
    )
```
